32 devices in a mesh: tensor: 4 (over z), mirror: 2 (over core), dp: 4 (over y, x).
Axes of the slice: x: 2, y: 2, z: 4, core: 2. Of those that a mesh axis runs over, the one named last changes fastest.
Arguments:
- layer_input: bfloat16 [8, 256, 4096], P(('mirror', 'dp'), 'tensor'), may hold values from -6 to 6
- qk_weight: bfloat16 [4096, 2, 4096], P(None, None, 'tensor'), may hold values from -0.09375 to 0.09375
- query_proj: bfloat16 [8, 256, 4096], P(('mirror', 'dp'), None, 'tensor'), may hold values from -24 to 24
- key_proj: bfloat16 [8, 256, 4096], P(('mirror', 'dp'), None, 'tensor'), may hold values from -24 to 24
- value_proj: bfloat16 [8, 256, 4096], P(('mirror', 'dp'), None, 'tensor'), may hold values from -6 to 6
- head_grad: bfloat16 [8, 256, 4096], P(('mirror', 'dp'), None, 'tensor'), may hold values from -6 to 6
- doc_ids: int32 [8, 256], P(('mirror', 'dp')), may hold values from 0 to 3, as said below
Outputs:
- input_grad: bfloat16 [8, 256, 4096], P(('mirror', 'dp'), 'tensor')
- qk_weight_grad: float32 [4096, 2, 4096], P(('mirror', 'dp'), None, 'tensor')
The draws below stay inside these ranges and needn't reach their ends.
Inputs may be any that keep to these rules, and one draw needn't show every extreme that they name: `doc_ids`: within each sequence of 128 tokens the ids start at 0, never fall, and each of the four documents holds a multiple of 8 tokens.
All inputs are finite; a program needn't handle non-finite values.
Results may differ from the reference program's by a relative error of at most 0.023.
Values may be sent and summed in bfloat16 or wider, within the bound.
No kernel may reach another device: no remote copies, remote signals or barrier semaphores. Data moves between devices by JAX's collectives and lax.ppermute only.
A program may use at most 128 MiB of HBM per device.

```python
import math
import jax
import jax.numpy as jnp
from jax import lax

D = 4096
HD = 128
SEQ = 128
MICRO = 2
TOK_DEV = 256
REPL = 8
N_TENSOR = 4


def document_ids(key_base):
    sequences = REPL * MICRO
    granule = SEQ // 16
    ranked = jax.random.randint(key_base, (sequences, 15), 0, 1 << 20) * 16 + jnp.arange(15)
    chosen = jnp.argsort(ranked, axis=1)[:, :3]
    cut_points = (chosen + 1) * granule
    positions = jnp.arange(SEQ)
    doc_index = jnp.sum((positions[None, :, None] >= cut_points[:, None, :]).astype(jnp.int32), axis=2)
    return doc_index.astype(jnp.int32).reshape(REPL, TOK_DEV)


def draw_doc_ids(key, part):
    return document_ids(jax.random.fold_in(key, 11))


def drawn_field(key, salt):
    base_field = jnp.clip(jax.random.normal(jax.random.fold_in(key, salt), (REPL, TOK_DEV, D), jnp.float32), -6.0, 6.0)
    return base_field


def draw_query_proj(key, part):
    return drawn_field(key, 21).astype(jnp.bfloat16)


def draw_key_proj(key, part):
    return drawn_field(key, 22).astype(jnp.bfloat16)


def strengthened(array, stream_key, source, target, blocks, factor):
    def block_of(position):
        return (jnp.arange(array.shape[position]) // (array.shape[position] // blocks)).reshape((-1,) + (1,) * (array.ndim - 1 - position))

    near = jax.random.permutation(stream_key, blocks)[block_of(target)]
    far = (block_of(target) + blocks // 2) % blocks
    return jnp.where((block_of(source) == near) | (block_of(source) == far), factor * array, array)


def levels(stream_key, dims, split, smallest, largest):
    level = 1.0
    for axis_at, parts in split:
        heights = jax.random.uniform(jax.random.fold_in(jax.random.fold_in(stream_key, 6), axis_at), (parts,), jnp.float32, smallest / len(split), largest / len(split))
        level = level * jnp.repeat(jnp.exp(heights), dims[axis_at] // parts).reshape((-1,) + (1,) * (len(dims) - 1 - axis_at))
    return level


def centred(rng, dims, spread, limit, cuts=(), kind=jnp.bfloat16):
    result = spread * jax.random.normal(rng, dims, jnp.float32)
    if cuts:
        result = result * levels(rng, dims, cuts, -0.22, 0.18)
    return jnp.clip(result, -limit, limit).astype(kind)


def gaussian_with(rng, dims, deviation, bound, pieces, heavy, held_as=jnp.bfloat16):
    entries = deviation * jax.random.normal(rng, dims, jnp.float32)
    if pieces:
        entries = entries * levels(rng, dims, pieces, -0.22, 0.18)
    return jnp.clip(strengthened(entries, jax.random.fold_in(rng, 3), *heavy), -bound, bound).astype(held_as)


def setup_inputs(seed: int = 0) -> dict:
    splits = jax.random.split(jax.random.key(seed), 8)
    layer_input = gaussian_with(splits[0], (REPL, TOK_DEV, D), 1.0, 6.0, ((0, 8), (1, 4)), (0, 2, 8, 2.0))
    qk_weight = centred(splits[1], (D, 2, D), D ** -0.5, 0.09375, ((2, 4),))
    query_proj = draw_query_proj(jax.random.fold_in(splits[7], 71), 0)
    key_proj = draw_key_proj(jax.random.fold_in(splits[7], 71), 0)
    value_proj = centred(splits[4], (REPL, TOK_DEV, D), 1.0, 6.0, ((0, 8), (2, 4)))
    head_grad = centred(splits[5], (REPL, TOK_DEV, D), 1.0, 6.0, ((0, 8), (2, 4)))
    doc_ids = draw_doc_ids(jax.random.fold_in(splits[7], 71), 0)
    return {"layer_input": layer_input, "qk_weight": qk_weight, "query_proj": query_proj, "key_proj": key_proj, "value_proj": value_proj, "head_grad": head_grad, "doc_ids": doc_ids}


def rotate_pairs(values, cosine, sine_table):
    half = values.shape[-1] // 2
    first_half = values[..., :half]
    second_half = values[..., half:]
    cos_b = cosine[None, :, None, :]
    sin_b = sine_table[None, :, None, :]
    return jnp.concatenate([first_half * cos_b - second_half * sin_b, second_half * cos_b + first_half * sin_b], axis=-1)

def unrotate_pairs(values, cosine, sine_table):
    half = values.shape[-1] // 2
    first_half = values[..., :half]
    second_half = values[..., half:]
    cos_b = cosine[None, :, None, :]
    sin_b = sine_table[None, :, None, :]
    return jnp.concatenate([first_half * cos_b + second_half * sin_b, second_half * cos_b - first_half * sin_b], axis=-1)

def attention_grads(query_rows, key_rows, value_rows, grad_rows, doc_row):
    token_count, full_width = query_rows.shape
    head_count = full_width // HD
    micro_count = token_count // SEQ
    shape_four = (micro_count, SEQ, head_count, HD)
    positions = jnp.arange(SEQ).astype(jnp.float32)
    inverse = jnp.exp(-(2.0 * jnp.arange(HD // 2).astype(jnp.float32) / HD) * math.log(10000.0))
    angles = positions[:, None] * inverse[None, :]
    cosine = jnp.cos(angles)
    sine_table = jnp.sin(angles)
    q_rot = rotate_pairs(query_rows.reshape(shape_four).astype(jnp.float32), cosine, sine_table).astype(jnp.bfloat16)
    k_rot = rotate_pairs(key_rows.reshape(shape_four).astype(jnp.float32), cosine, sine_table).astype(jnp.bfloat16)
    scale = 1.0 / math.sqrt(HD)
    scores = jnp.einsum('bshd,bthd->bhst', q_rot.astype(jnp.float32), k_rot.astype(jnp.float32)) * scale
    docs = doc_row.reshape(micro_count, SEQ)
    index_seq = jnp.arange(SEQ)
    causal = index_seq[None, :] <= index_seq[:, None]
    allowed = causal[None, :, :] & (docs[:, :, None] == docs[:, None, :])
    scores = jnp.where(allowed[:, None, :, :], scores, -1e+30)
    highest = lax.optimization_barrier(jnp.max(scores, axis=-1, keepdims=True))
    exps = jnp.exp(scores - highest)
    probs = exps / lax.optimization_barrier(jnp.sum(exps, axis=-1, keepdims=True))
    dprob = jnp.einsum('bshd,bthd->bhst', grad_rows.reshape(shape_four).astype(jnp.float32), value_rows.reshape(shape_four).astype(jnp.float32))
    delta = lax.optimization_barrier(jnp.sum(probs * dprob, axis=-1, keepdims=True))
    dscore = (probs * (dprob - delta)).astype(jnp.bfloat16)
    dq_rot = jnp.einsum('bhst,bthd->bshd', dscore.astype(jnp.float32), k_rot.astype(jnp.float32)) * scale
    dk_rot = jnp.einsum('bhst,bshd->bthd', dscore.astype(jnp.float32), q_rot.astype(jnp.float32)) * scale
    query_grad = unrotate_pairs(dq_rot, cosine, sine_table).astype(jnp.bfloat16).reshape(token_count, full_width)
    key_grad = unrotate_pairs(dk_rot, cosine, sine_table).astype(jnp.bfloat16).reshape(token_count, full_width)
    return (query_grad, key_grad)

def reference(layer_input, qk_weight, query_proj, key_proj, value_proj, head_grad, doc_ids):
    group_width = D // N_TENSOR
    weight_groups = qk_weight.astype(jnp.float32).reshape(D, 2, N_TENSOR, group_width)

    def replica_step(accumulated, slices_in):
        inputs_rows, query_rows, key_rows, value_rows, grad_rows, doc_row = slices_in
        query_grad, key_grad = attention_grads(query_rows, key_rows, value_rows, grad_rows, doc_row)
        stacked = jnp.stack([query_grad, key_grad], axis=1).astype(jnp.float32)
        partials = jnp.einsum('tjnc,djnc->ntd', stacked.reshape(TOK_DEV, 2, N_TENSOR, group_width), weight_groups)
        partials = lax.optimization_barrier(partials.astype(jnp.bfloat16)).astype(jnp.float32)
        input_rows = lax.optimization_barrier(jnp.sum(partials, axis=0)).astype(jnp.bfloat16)
        term = jnp.einsum('ti,tjc->ijc', inputs_rows.astype(jnp.float32), stacked)
        term = lax.optimization_barrier(term.astype(jnp.bfloat16)).astype(jnp.float32)
        return (accumulated + term, input_rows)
    start_sum = jnp.zeros((D, 2, D), jnp.float32)
    accumulated, input_grad = lax.scan(replica_step, start_sum, (layer_input, query_proj, key_proj, value_proj, head_grad, doc_ids))
    return (input_grad, accumulated / REPL)
```

```python
import functools
import math

import jax
import jax.numpy as jnp
import numpy as np
from jax import lax
from jax.experimental import pallas as pl
from jax.experimental.pallas import tpu as pltpu
from jax.sharding import PartitionSpec as P

HD = 128
SEQ = 128
VMEM_LIMIT = 48 << 20
ROWS = (((1,), (1,)), ((), ()))
COLS = (((0,), (0,)), ((), ()))


def rope_tables():
    half = HD // 2
    inverse = np.exp(-(np.float32(2.0) * np.arange(half, dtype=np.float32) / np.float32(HD)) * np.float32(math.log(10000.0)))
    angles = np.arange(SEQ, dtype=np.float32)[:, None] * inverse[None, :].astype(np.float32)
    cosine, sine = np.cos(angles), np.sin(angles)
    return np.concatenate([cosine, cosine], axis=1), np.concatenate([-sine, sine], axis=1)


def attention_kernel(doc_ref, cos_ref, sin_ref, q_ref, k_ref, v_ref, h_ref, qg_ref, kg_ref):
    cosine, sine = cos_ref[...], sin_ref[...]
    scale = 1.0 / math.sqrt(HD)
    keys = lax.broadcast_in_dim(doc_ref[0], (SEQ, SEQ), (0, 1))
    row = lax.broadcasted_iota(jnp.int32, (SEQ, SEQ), 0)
    col = lax.broadcasted_iota(jnp.int32, (SEQ, SEQ), 1)
    allowed = (col <= row) & (keys == keys.T)

    def rope(values):
        values = values.astype(jnp.float32)
        return (values * cosine + pltpu.roll(values, HD // 2, 1) * sine).astype(jnp.bfloat16)

    def unrope(values):
        values = values * scale
        return (values * cosine - pltpu.roll(values, HD // 2, 1) * sine).astype(jnp.bfloat16)

    for head in range(q_ref.shape[1] // HD):
        at = slice(head * HD, (head + 1) * HD)
        q_rot, k_rot = rope(q_ref[:, at]), rope(k_ref[:, at])
        scores = lax.dot_general(q_rot, k_rot, ROWS, preferred_element_type=jnp.float32) * scale
        scores = jnp.where(allowed, scores, -1e30)
        exps = jnp.exp(scores - jnp.max(scores, axis=1, keepdims=True))
        probs = exps / jnp.sum(exps, axis=1, keepdims=True)
        dprob = lax.dot_general(h_ref[:, at], v_ref[:, at], ROWS, preferred_element_type=jnp.float32)
        delta = jnp.sum(probs * dprob, axis=1, keepdims=True)
        dscore = (probs * (dprob - delta)).astype(jnp.bfloat16)
        qg_ref[:, at] = unrope(jnp.dot(dscore, k_rot, preferred_element_type=jnp.float32))
        kg_ref[:, at] = unrope(lax.dot_general(dscore, q_rot, COLS, preferred_element_type=jnp.float32))


def attention_grads(query, key, value, grad, docs):
    tokens, width = query.shape
    micro = tokens // SEQ
    split = 2 if (width // HD) % 2 == 0 else 1
    cosine, sine = rope_tables()
    table = pl.BlockSpec((SEQ, HD), lambda b, h: (0, 0))
    block = pl.BlockSpec((SEQ, width // split), lambda b, h: (b, h))
    return pl.pallas_call(
        attention_kernel,
        grid=(micro, split),
        in_specs=[pl.BlockSpec((1, 1, SEQ), lambda b, h: (b, 0, 0)), table, table] + [block] * 4,
        out_specs=[block, block],
        out_shape=[jax.ShapeDtypeStruct((tokens, width), jnp.bfloat16)] * 2,
        compiler_params=pltpu.CompilerParams(vmem_limit_bytes=VMEM_LIMIT),
        name="attention_grads",
    )(docs.reshape(micro, 1, SEQ), cosine, sine, query, key, value, grad)


def partials_kernel(qg_ref, kg_ref, w_ref, out_ref):
    depth, _, width = w_ref.shape
    weights = w_ref[...].reshape(depth, 2 * width)
    rows = lax.dot_general(qg_ref[...], weights[:, :width], ROWS, preferred_element_type=jnp.float32)
    rows = rows + lax.dot_general(kg_ref[...], weights[:, width:], ROWS, preferred_element_type=jnp.float32)
    out_ref[...] = rows.astype(jnp.bfloat16).reshape(out_ref.shape)


def input_partials(query_grad, key_grad, weight, owners, blocks):
    tokens, width = query_grad.shape
    model = weight.shape[0]
    columns = model // blocks
    depth = min(512, columns)
    per = columns // depth
    grads = pl.BlockSpec((tokens, width), lambda j: (0, 0))
    return pl.pallas_call(
        partials_kernel,
        grid=(model // depth,),
        in_specs=[grads, grads, pl.BlockSpec((depth, 2, width), lambda j: (j, 0, 0))],
        out_specs=pl.BlockSpec((owners, 1, tokens // owners, depth), lambda j: (0, j // per, 0, j % per)),
        out_shape=jax.ShapeDtypeStruct((owners, blocks, tokens // owners, columns), jnp.bfloat16),
        compiler_params=pltpu.CompilerParams(vmem_limit_bytes=VMEM_LIMIT),
        name="input_partials",
    )(query_grad, key_grad, weight)


def split_kernel(index_ref, x_ref, *out_refs):
    mirrors = index_ref.shape[0] - 1
    data_count = len(out_refs)
    width = x_ref.shape[1] // (mirrors * data_count)
    for distance, out_ref in enumerate(out_refs):
        owner = index_ref[mirrors] ^ distance
        for k in range(mirrors):
            start = pl.multiple_of((index_ref[k] * data_count + owner) * width, width)
            out_ref[:, k * width : (k + 1) * width] = x_ref[:, pl.ds(start, width)]


def split_columns(rows, mirrors, data_count):
    mirror = lax.axis_index("mirror")
    index = jnp.stack([(mirror + k) % mirrors for k in range(mirrors)] + [lax.axis_index("dp")])
    tokens, model = rows.shape
    out = jax.ShapeDtypeStruct((tokens, model // data_count), rows.dtype)
    return pl.pallas_call(
        split_kernel,
        in_specs=[pl.BlockSpec(memory_space=pltpu.SMEM), pl.BlockSpec(memory_space=pltpu.VMEM)],
        out_specs=[pl.BlockSpec(memory_space=pltpu.VMEM)] * data_count,
        out_shape=[out] * data_count,
        name="split_columns",
    )(index.astype(jnp.int32), rows)


def swap(values, distance, size):
    return lax.ppermute(values, "dp", [(i, i ^ distance) for i in range(size)])


def gathered(block, bits, size):
    blocks = {0: block}
    for bit in bits:
        blocks.update({d ^ bit: swap(b, bit, size) for d, b in list(blocks.items())})
    return [blocks[d] for d in range(size)]


def shards(layer_input, qk_weight, query_proj, key_proj, value_proj, head_grad, doc_ids):
    owners = lax.axis_size("tensor")
    mirrors = lax.axis_size("mirror")
    data_count = lax.axis_size("dp")
    tokens, width = query_proj.shape[1:]
    model = layer_input.shape[2]
    block_rows = model // (mirrors * data_count)
    own_tokens = tokens // owners
    me = lax.axis_index("tensor")

    columns = split_columns(layer_input[0], mirrors, data_count)
    columns = [columns[0]] + [swap(columns[d], d, data_count) for d in range(1, data_count)]
    piece = jnp.concatenate(columns, axis=0)

    query_grad, key_grad = attention_grads(
        query_proj[0], key_proj[0], value_proj[0], head_grad[0], doc_ids[0]
    )
    bits = [1 << b for b in range(data_count.bit_length() - 1)]
    query_all = gathered(query_grad, bits, data_count)
    key_all = gathered(key_grad, bits[1:] + bits[:1], data_count)

    partials = input_partials(query_grad, key_grad, qk_weight, owners, data_count)
    partials = partials.reshape(owners, *piece.shape)

    right = [(i, i + 1) for i in range(owners - 1)]
    left = [(i + 1, i) for i in range(owners - 1)]
    from_left, from_right = [piece], [piece]
    for slot in range(1, owners + 1):
        send_right, send_left = from_left[-1], from_right[-1]
        if slot > 1:
            ahead = owners - slot + 1
            term = lax.dynamic_index_in_dim(partials, jnp.minimum(me + ahead, owners - 1), 0, False)
            send_right = send_right + jnp.where(me + ahead < owners, term, jnp.zeros_like(term))
            term = lax.dynamic_index_in_dim(partials, jnp.maximum(me - ahead, 0), 0, False)
            send_left = send_left + jnp.where(me - ahead >= 0, term, jnp.zeros_like(term))
        from_left.append(lax.ppermute(send_right, "tensor", right))
        from_right.append(lax.ppermute(send_left, "tensor", left))
    own = lax.dynamic_index_in_dim(partials, me, 0, False).astype(jnp.float32)
    own = own + from_left[owners].astype(jnp.float32) + from_right[owners].astype(jnp.float32)
    own = own.astype(jnp.bfloat16).reshape(data_count, own_tokens, model // data_count)
    input_grad = jnp.swapaxes(own, 0, 1).reshape(1, own_tokens, model)

    pieces = [piece] + [
        jnp.where(me >= t, from_left[t], from_right[owners - t]) for t in range(1, owners)
    ]
    stacked = jnp.stack(pieces)
    stacked = jnp.take(stacked, (me - jnp.arange(owners)) % owners, axis=0)
    stacked = stacked.reshape(owners, data_count, own_tokens, mirrors * block_rows)
    inputs = jnp.swapaxes(stacked, 0, 1).reshape(data_count * tokens, mirrors * block_rows)

    halves = []
    for blocks in (query_all, key_all):
        grads = jnp.concatenate(blocks, axis=0)
        total = lax.dot_general(inputs, grads, COLS, preferred_element_type=jnp.float32)
        half = total[:block_rows]
        for k in range(1, mirrors):
            away = total[k * block_rows : (k + 1) * block_rows].astype(jnp.bfloat16)
            away = lax.ppermute(away, "mirror", [(i, (i + k) % mirrors) for i in range(mirrors)])
            half = half + away.astype(jnp.float32)
        halves.append(half / (mirrors * data_count))
    weight_grad = jnp.stack(halves, axis=1)
    return (input_grad, weight_grad)


def solution(mesh):
    in_specs = (
        P(("mirror", "dp"), "tensor", None),
        P(None, None, "tensor"),
        P(("mirror", "dp"), None, "tensor"),
        P(("mirror", "dp"), None, "tensor"),
        P(("mirror", "dp"), None, "tensor"),
        P(("mirror", "dp"), None, "tensor"),
        P(("mirror", "dp"), None),
    )
    out_specs = (P(("mirror", "dp"), "tensor", None), P(("mirror", "dp"), None, "tensor"))
    return jax.shard_map(shards, mesh=mesh, in_specs=in_specs, out_specs=out_specs, check_vma=False)
```

```python
import functools
import math

import jax
import jax.numpy as jnp
import numpy as np
from jax import lax
from jax.experimental import pallas as pl
from jax.experimental.pallas import tpu as pltpu
from jax.sharding import PartitionSpec as P

HD = 128
SEQ = 128
GROUP = 4
MIB = 1 << 20
ROWS = (((1,), (1,)), ((), ()))
COLS = (((0,), (0,)), ((), ()))
NEAR = pl.BlockSpec(memory_space=pltpu.VMEM)
FAR = pl.BlockSpec(memory_space=pl.ANY)


def params(mib):
    return pltpu.CompilerParams(vmem_limit_bytes=mib * MIB)


def rope_tables():
    half = HD // 2
    inverse = np.exp(-(np.float32(2.0) * np.arange(half, dtype=np.float32) / np.float32(HD)) * np.float32(math.log(10000.0)))
    angles = np.arange(SEQ, dtype=np.float32)[:, None] * inverse[None, :].astype(np.float32)
    cosine, sine = np.cos(angles), np.sin(angles)
    return np.stack([np.concatenate([cosine, cosine], axis=1), np.concatenate([-sine, sine], axis=1)])


def attention_kernel(doc_ref, table_ref, q_ref, k_ref, v_ref, h_ref, grad_ref, in_s, in_sem):
    tokens, width = q_ref.shape
    scale = 1.0 / math.sqrt(HD)
    loads = []
    for b in range(tokens // SEQ):
        at = pl.ds(b * SEQ, SEQ)
        refs = enumerate((q_ref, k_ref, v_ref, h_ref))
        loads.append([pltpu.make_async_copy(ref.at[at], in_s.at[i, at], in_sem.at[b, i]) for i, ref in refs])
    for copy in [c for load in loads for c in load]:
        copy.start()

    cosine, sine = table_ref[0], table_ref[1]
    back_cosine, back_sine = cosine * scale, sine * scale
    row = lax.broadcasted_iota(jnp.int32, (SEQ, SEQ), 0)
    col = lax.broadcasted_iota(jnp.int32, (SEQ, SEQ), 1)

    def rope(values):
        values = values.astype(jnp.float32)
        return (values * cosine + pltpu.roll(values, HD // 2, 1) * sine).astype(jnp.bfloat16)

    def unrope(values):
        return (values * back_cosine - pltpu.roll(values, HD // 2, 1) * back_sine).astype(jnp.bfloat16)

    for b in range(tokens // SEQ):
        rows = slice(b * SEQ, (b + 1) * SEQ)
        queries = lax.broadcast_in_dim(doc_ref[b], (SEQ, SEQ), (0, 1))
        allowed = (row <= col) & (queries == queries.T)
        for copy in loads[b]:
            copy.wait()
        for first in range(0, width // HD, GROUP):
            ats = [slice(h * HD, (h + 1) * HD) for h in range(first, min(first + GROUP, width // HD))]
            q_rot = [rope(in_s[0, rows, at]) for at in ats]
            k_rot = [rope(in_s[1, rows, at]) for at in ats]
            scores = [
                lax.dot_general(k, q, ROWS, preferred_element_type=jnp.float32) for q, k in zip(q_rot, k_rot)
            ]
            dprob = [
                lax.dot_general(in_s[2, rows, at], in_s[3, rows, at], ROWS, preferred_element_type=jnp.float32)
                for at in ats
            ]
            scores = [jnp.where(allowed, s, -1e30) for s in scores]
            exps = [
                jnp.exp2((s - jnp.max(s, axis=0, keepdims=True)) * (scale * math.log2(math.e))) for s in scores
            ]
            probs = [e * (1.0 / jnp.sum(e, axis=0, keepdims=True)) for e in exps]
            dscore = [
                (p * (d - jnp.sum(p * d, axis=0, keepdims=True))).astype(jnp.bfloat16)
                for p, d in zip(probs, dprob)
            ]
            for at, ds, q, k in zip(ats, dscore, q_rot, k_rot):
                grad_ref[0, rows, at] = unrope(lax.dot_general(ds, k, COLS, preferred_element_type=jnp.float32))
                grad_ref[1, rows, at] = unrope(jnp.dot(ds, q, preferred_element_type=jnp.float32))


def attention_grads(query, key, value, grad, docs):
    tokens, width = query.shape
    micro = tokens // SEQ
    return pl.pallas_call(
        attention_kernel,
        in_specs=[NEAR, NEAR] + [FAR] * 4,
        out_specs=NEAR,
        out_shape=jax.ShapeDtypeStruct((2, tokens, width), jnp.bfloat16),
        scratch_shapes=[
            pltpu.VMEM((4, tokens, width), jnp.bfloat16),
            pltpu.SemaphoreType.DMA((micro, 4)),
        ],
        compiler_params=params(56),
        name="attention_grads",
    )(docs.reshape(micro, 1, SEQ), rope_tables(), query, key, value, grad)


def partials_kernel(pieces, grad_ref, w_ref, out_ref, w_s, out_s, w_sem, out_sem):
    owners, blocks, own_tokens, columns = out_ref.shape
    width = w_ref.shape[2]
    depth = columns // pieces
    fetches = []
    for c in range(blocks * pieces):
        at = pl.ds(c * depth, depth)
        fetches.append(pltpu.make_async_copy(w_ref.at[at], w_s.at[at], w_sem.at[c]))
    for copy in fetches:
        copy.start()
    stores = []
    for block in range(blocks):
        for copy in fetches[block * pieces : (block + 1) * pieces]:
            copy.wait()
        weights = w_s[block * columns : (block + 1) * columns].reshape(columns, 2 * width)
        out = lax.dot_general(grad_ref[0], weights[:, :width], ROWS, preferred_element_type=jnp.float32)
        out = out + lax.dot_general(grad_ref[1], weights[:, width:], ROWS, preferred_element_type=jnp.float32)
        out_s[:, block] = out.astype(jnp.bfloat16).reshape(owners, own_tokens, columns)
        stores.append(pltpu.make_async_copy(out_s.at[:, block], out_ref.at[:, block], out_sem.at[block]))
        stores[-1].start()
    for copy in stores:
        copy.wait()


def input_partials(grads, weight, owners, blocks):
    _, tokens, width = grads.shape
    model = weight.shape[0]
    pieces = 2
    shape = (owners, blocks, tokens // owners, model // blocks)
    return pl.pallas_call(
        functools.partial(partials_kernel, pieces),
        in_specs=[NEAR, FAR],
        out_specs=FAR,
        out_shape=jax.ShapeDtypeStruct(shape, jnp.bfloat16),
        scratch_shapes=[
            pltpu.VMEM(weight.shape, jnp.bfloat16),
            pltpu.VMEM(shape, jnp.bfloat16),
            pltpu.SemaphoreType.DMA((blocks * pieces,)),
            pltpu.SemaphoreType.DMA((blocks,)),
        ],
        compiler_params=params(52),
        name="input_partials",
    )(grads, weight)


def split_kernel(mirrors, x_ref, *refs):
    out_refs, sem = refs[:-1], refs[-1]
    data_count = len(out_refs)
    width = x_ref.shape[1] // (mirrors * data_count)
    copies = []
    for distance, out_ref in enumerate(out_refs):
        owner = lax.axis_index("dp") ^ distance
        for k in range(mirrors):
            block = lax.rem(lax.axis_index("mirror") + k, mirrors) * data_count + owner
            source = x_ref.at[:, pl.ds(pl.multiple_of(block * width, width), width)]
            target = out_ref.at[:, pl.ds(k * width, width)]
            copies.append(pltpu.make_async_copy(source, target, sem.at[distance, k]))
    for copy in copies:
        copy.start()
    for copy in copies:
        copy.wait()


def split_columns(rows, mirrors, data_count):
    tokens, model = rows.shape
    out = jax.ShapeDtypeStruct((tokens, model // data_count), rows.dtype)
    return pl.pallas_call(
        functools.partial(split_kernel, mirrors),
        in_specs=[FAR],
        out_specs=[FAR] * data_count,
        out_shape=[out] * data_count,
        scratch_shapes=[pltpu.SemaphoreType.DMA((data_count, mirrors))],
        compiler_params=params(16),
        name="split_columns",
    )(rows)


def merge_kernel(*refs):
    in_refs, out_ref = refs[:-1], refs[-1]
    tokens = in_refs[0].shape[0]
    for i, in_ref in enumerate(in_refs):
        out_ref[i * tokens : (i + 1) * tokens, :] = in_ref[...]


def merge_tokens(columns):
    tokens, width = columns[0].shape
    return pl.pallas_call(
        merge_kernel,
        in_specs=[NEAR] * len(columns),
        out_specs=NEAR,
        out_shape=jax.ShapeDtypeStruct((len(columns) * tokens, width), columns[0].dtype),
        compiler_params=params(16),
        name="merge_tokens",
    )(*columns)


def hop(values, parity, size):
    pairs = []
    for i in range(size):
        j = i + 1 if i % 2 == parity else i - 1
        pairs.append((i, j if 0 <= j < size else i))
    return lax.ppermute(values, "tensor", pairs)


def has_partner(me, parity, size):
    ahead = lax.rem(me, 2) == parity
    partner = jnp.where(ahead, me + 1, me - 1)
    return (partner >= 0) & (partner < size), ahead


def pass_kernel(parity, distance, flow_ref, part_ref, out_ref, part_s, sem):
    size = part_ref.shape[0]
    me = lax.axis_index("tensor")
    ahead = lax.rem(me, 2) == parity
    owner = jnp.where(ahead, me + distance, me - distance)
    active = (owner >= 0) & (owner < size)
    flows, _ = has_partner(me, 1 - parity, size)
    copy = pltpu.make_async_copy(part_ref.at[jnp.clip(owner, 0, size - 1)], part_s, sem)
    copy.start()
    copy.wait()

    @pl.when(flows & active)
    def _():
        out_ref[...] = flow_ref[...] + part_s[...]

    @pl.when(jnp.logical_not(flows))
    def _():
        out_ref[...] = part_s[...]

    @pl.when(flows & jnp.logical_not(active))
    def _():
        out_ref[...] = flow_ref[...]


def pass_on(flow, partials, parity, distance):
    return pl.pallas_call(
        functools.partial(pass_kernel, parity, distance),
        in_specs=[NEAR, FAR],
        out_specs=NEAR,
        out_shape=jax.ShapeDtypeStruct(flow.shape, flow.dtype),
        scratch_shapes=[pltpu.VMEM(flow.shape, flow.dtype), pltpu.SemaphoreType.DMA(())],
        compiler_params=params(16),
        name="pass_on",
    )(flow, partials)


def finish_kernel(blocks, even_ref, odd_ref, part_ref, out_ref, part_s, sem):
    size = part_ref.shape[0]
    me = lax.axis_index("tensor")
    copy = pltpu.make_async_copy(part_ref.at[me], part_s, sem)
    copy.start()
    copy.wait()
    tokens, columns = out_ref.shape[0], out_ref.shape[1] // blocks

    def store(total):
        for block in range(blocks):
            rows = total[block * tokens : (block + 1) * tokens]
            out_ref[:, block * columns : (block + 1) * columns] = rows.astype(out_ref.dtype)

    for parity, (flow_ref, other_ref) in enumerate(((odd_ref, even_ref), (even_ref, odd_ref))):
        alone = jnp.logical_not(has_partner(me, 1 - parity, size)[0])

        @pl.when(alone)
        def _(other_ref=other_ref):
            store(part_s[...].astype(jnp.float32) + other_ref[...].astype(jnp.float32))

    both = has_partner(me, 0, size)[0] & has_partner(me, 1, size)[0]

    @pl.when(both)
    def _():
        total = part_s[...].astype(jnp.float32) + even_ref[...].astype(jnp.float32)
        store(total + odd_ref[...].astype(jnp.float32))


def finish(even, odd, partials, blocks):
    rows, columns = even.shape
    return pl.pallas_call(
        functools.partial(finish_kernel, blocks),
        in_specs=[NEAR, NEAR, FAR],
        out_specs=NEAR,
        out_shape=jax.ShapeDtypeStruct((rows // blocks, columns * blocks), even.dtype),
        scratch_shapes=[pltpu.VMEM(even.shape, even.dtype), pltpu.SemaphoreType.DMA(())],
        compiler_params=params(16),
        name="finish_input_grad",
    )(even, odd, partials)


def weight_kernel(counts, places, *refs):
    size, data_count, side, away = counts
    pieces = 2 * size - 1
    piece_refs, grad_refs = refs[:pieces], refs[pieces:-5]
    out_ref, x_s, grad_s, x_sem, grad_sem = refs[-5:]
    own_ref, even_refs, odd_refs = piece_refs[0], piece_refs[1 : size], piece_refs[size:]
    me = lax.axis_index("tensor")
    tokens = x_s.shape[0] // data_count
    own_tokens = tokens // size
    rows, width = x_s.shape[1], grad_s.shape[2]

    def fetch(ref, slot, k):
        owner = lax.rem(me - slot + size, size)
        start = pl.multiple_of(k * tokens + owner * own_tokens, own_tokens)
        source = ref.at[pl.ds(k * own_tokens, own_tokens), pl.ds(side * rows, rows)]
        return pltpu.make_async_copy(source, x_s.at[pl.ds(start, own_tokens)], x_sem.at[slot, k])

    odd_place = lax.rem(me, 2) == 1
    for k in range(data_count):
        fetch(own_ref, 0, k).start()
    for slot in range(1, size):
        behind = me >= slot
        came = (
            (behind & odd_place, even_refs[slot - 1]),
            (behind & jnp.logical_not(odd_place), odd_refs[slot - 1]),
            (jnp.logical_not(behind) & odd_place, odd_refs[size - slot - 1]),
            (jnp.logical_not(behind) & jnp.logical_not(odd_place), even_refs[size - slot - 1]),
        )
        for condition, ref in came:

            @pl.when(condition)
            def _(ref=ref, slot=slot):
                for k in range(data_count):
                    fetch(ref, slot, k).start()

    loads = []
    for j in range(2):
        for k in range(data_count):
            which, half = places[k][j]
            source = grad_refs[which] if half is None else grad_refs[which].at[half]
            target = grad_s.at[j, pl.ds(k * tokens, tokens)]
            loads.append(pltpu.make_async_copy(source, target, grad_sem.at[j, k]))
    for copy in loads:
        copy.start()
    for slot in range(size):
        for k in range(data_count):
            fetch(own_ref, slot, k).wait()
    for j in range(2):
        for copy in loads[j * data_count : (j + 1) * data_count]:
            copy.wait()
        total = lax.dot_general(x_s[...], grad_s[j], COLS, preferred_element_type=jnp.float32)
        out_ref[:, j * width : (j + 1) * width] = total.astype(out_ref.dtype)


def weight_sums(own, even, odd, grads, mirrors, side, dtype):
    size, data_count = len(even) + 1, len(grads)
    rows = own.shape[1] // mirrors
    arrays, places = [], []
    for pair in grads:
        place = []
        for array, half in pair:
            if not any(array is a for a in arrays):
                arrays.append(array)
            place.append(([i for i, a in enumerate(arrays) if a is array][0], half))
        places.append(place)
    tokens, width = arrays[0].shape[-2:]
    pieces = [own] + even + odd
    return pl.pallas_call(
        functools.partial(weight_kernel, (size, data_count, side, mirrors), places),
        in_specs=[FAR] * (len(pieces) + len(arrays)),
        out_specs=NEAR,
        out_shape=jax.ShapeDtypeStruct((rows, 2 * width), dtype),
        scratch_shapes=[
            pltpu.VMEM((data_count * tokens, rows), jnp.bfloat16),
            pltpu.VMEM((2, data_count * tokens, width), jnp.bfloat16),
            pltpu.SemaphoreType.DMA((size, data_count)),
            pltpu.SemaphoreType.DMA((2, data_count)),
        ],
        compiler_params=params(32),
        name="weight_sums",
    )(*pieces, *arrays)


def average_kernel(replicas, own_ref, *refs):
    away_refs, out_ref = refs[:-1], refs[-1]
    total = own_ref[...]
    for away_ref in away_refs:
        total = total + away_ref[...].astype(jnp.float32)
    out_ref[...] = (total * (1.0 / replicas)).reshape(out_ref.shape)


def average(own, away, replicas):
    rows, columns = own.shape
    depth = min(rows, 128)
    block = pl.BlockSpec((depth, columns), lambda i: (i, 0))
    return pl.pallas_call(
        functools.partial(average_kernel, replicas),
        grid=(rows // depth,),
        in_specs=[block] * (1 + len(away)),
        out_specs=pl.BlockSpec((depth, 2, columns // 2), lambda i: (i, 0, 0)),
        out_shape=jax.ShapeDtypeStruct((rows, 2, columns // 2), jnp.float32),
        compiler_params=params(32),
        name="average_weight_grad",
    )(own, *away)


def swap(values, distance, size):
    return lax.ppermute(values, "dp", [(i, i ^ distance) for i in range(size)])


def across(values, distance, size):
    return lax.ppermute(values, "mirror", [(i, (i + distance) % size) for i in range(size)])


def gathered(grads, size):
    bits = [1 << b for b in range(size.bit_length() - 1)]
    near = {bit: swap(grads, bit, size) for bit in bits}
    found = []
    for half, order in enumerate((bits, bits[1:] + bits[:1])):
        blocks = {0: (grads, half)}
        for bit in order:
            for distance, (array, part) in list(blocks.items()):
                if distance == 0:
                    blocks[bit] = (near[bit], half)
                else:
                    moved = array if part is None else array[part]
                    blocks[distance ^ bit] = (swap(moved, bit, size), None)
        found.append(blocks)
    return [(found[0][d], found[1][d]) for d in range(size)]


def shards(layer_input, qk_weight, query_proj, key_proj, value_proj, head_grad, doc_ids):
    size = lax.axis_size("tensor")
    mirrors = lax.axis_size("mirror")
    data_count = lax.axis_size("dp")

    columns = split_columns(layer_input[0], mirrors, data_count)
    columns = [columns[0]] + [swap(columns[d], d, data_count) for d in range(1, data_count)]
    grads = attention_grads(query_proj[0], key_proj[0], value_proj[0], head_grad[0], doc_ids[0])
    columns, grads = lax.optimization_barrier((columns, grads))
    piece = merge_tokens(columns)

    gathered_grads = gathered(grads, data_count)
    partials = input_partials(grads, qk_weight, size, data_count)
    partials = partials.reshape(size, *piece.shape)

    even, odd = [hop(piece, 0, size)], [hop(piece, 1, size)]
    for distance in range(size - 1, 0, -1):
        send_even = pass_on(odd[-1], partials, 0, distance)
        send_odd = pass_on(even[-1], partials, 1, distance)
        even.append(hop(send_even, 0, size))
        odd.append(hop(send_odd, 1, size))
    input_grad = finish(even[-1], odd[-1], partials, data_count)[None]

    away = []
    for r in range(1, mirrors):
        sums = weight_sums(piece, even[:-1], odd[:-1], gathered_grads, mirrors, r, jnp.bfloat16)
        away.append(across(sums, r, mirrors))
    own = weight_sums(piece, even[:-1], odd[:-1], gathered_grads, mirrors, 0, jnp.float32)
    weight_grad = average(own, away, mirrors * data_count)
    return (input_grad, weight_grad)


def solution(mesh):
    in_specs = (
        P(("mirror", "dp"), "tensor", None),
        P(None, None, "tensor"),
        P(("mirror", "dp"), None, "tensor"),
        P(("mirror", "dp"), None, "tensor"),
        P(("mirror", "dp"), None, "tensor"),
        P(("mirror", "dp"), None, "tensor"),
        P(("mirror", "dp"), None),
    )
    out_specs = (P(("mirror", "dp"), "tensor", None), P(("mirror", "dp"), None, "tensor"))
    return jax.shard_map(shards, mesh=mesh, in_specs=in_specs, out_specs=out_specs, check_vma=False)
```

```python
import functools
import math

import jax
import jax.numpy as jnp
import numpy as np
from jax import lax
from jax.experimental import pallas as pl
from jax.experimental.pallas import tpu as pltpu
from jax.sharding import PartitionSpec as P

HD = 128
SEQ = 128
GROUP = 4
SPAN = 1024
MIB = 1 << 20
ROWS = (((1,), (1,)), ((), ()))
COLS = (((0,), (0,)), ((), ()))
BRIEF = pl.CostEstimate(flops=1, bytes_accessed=1, transcendentals=0)
NEAR = pl.BlockSpec(memory_space=pltpu.VMEM)
FAR = pl.BlockSpec(memory_space=pl.ANY)


def params(mib):
    return pltpu.CompilerParams(vmem_limit_bytes=mib * MIB)


def in_hbm(array):
    return pltpu.with_memory_space_constraint(array, pltpu.HBM)


def rope_tables():
    half = HD // 2
    inverse = np.exp(-(np.float32(2.0) * np.arange(half, dtype=np.float32) / np.float32(HD)) * np.float32(math.log(10000.0)))
    angles = np.arange(SEQ, dtype=np.float32)[:, None] * inverse[None, :].astype(np.float32)
    cosine, sine = np.cos(angles), np.sin(angles)
    return np.stack([np.concatenate([cosine, cosine], axis=1), np.concatenate([-sine, sine], axis=1)])


def attention_kernel(doc_ref, table_ref, q_ref, k_ref, v_ref, h_ref, w_ref, grad_ref, near_ref, doc_s, table_s, in_s, doc_sem, in_sem, w_sem):
    tokens, width = q_ref.shape
    scale = 1.0 / math.sqrt(HD)
    loads = []
    for b in range(tokens // SEQ):
        at = pl.ds(b * SEQ, SEQ)
        refs = enumerate((q_ref, k_ref, v_ref, h_ref))
        loads.append([pltpu.make_async_copy(ref.at[at], in_s.at[i, at], in_sem.at[b, i]) for i, ref in refs])
    first = [pltpu.make_async_copy(doc_ref, doc_s, doc_sem.at[0]), pltpu.make_async_copy(table_ref, table_s, doc_sem.at[1])]
    fetch = pltpu.make_async_copy(w_ref.at[pl.ds(0, near_ref.shape[0])], near_ref, w_sem)
    for copy in first + [c for load in loads for c in load] + [fetch]:
        copy.start()
    for copy in first:
        copy.wait()

    cosine, sine = table_s[0], table_s[1]
    back_cosine, back_sine = cosine * scale, sine * scale
    row = lax.broadcasted_iota(jnp.int32, (SEQ, SEQ), 0)
    col = lax.broadcasted_iota(jnp.int32, (SEQ, SEQ), 1)

    def rope(values):
        values = values.astype(jnp.float32)
        return (values * cosine + pltpu.roll(values, HD // 2, 1) * sine).astype(jnp.bfloat16)

    def unrope(values):
        return (values * back_cosine - pltpu.roll(values, HD // 2, 1) * back_sine).astype(jnp.bfloat16)

    for b in range(tokens // SEQ):
        rows = slice(b * SEQ, (b + 1) * SEQ)
        queries = lax.broadcast_in_dim(doc_s[b], (SEQ, SEQ), (0, 1))
        allowed = (row <= col) & (queries == queries.T)
        for copy in loads[b]:
            copy.wait()
        for first in range(0, width // HD, GROUP):
            ats = [slice(h * HD, (h + 1) * HD) for h in range(first, min(first + GROUP, width // HD))]
            q_rot = [rope(in_s[0, rows, at]) for at in ats]
            k_rot = [rope(in_s[1, rows, at]) for at in ats]
            scores = [
                lax.dot_general(k, q, ROWS, preferred_element_type=jnp.float32) for q, k in zip(q_rot, k_rot)
            ]
            dprob = [
                lax.dot_general(in_s[2, rows, at], in_s[3, rows, at], ROWS, preferred_element_type=jnp.float32)
                for at in ats
            ]
            scores = [jnp.where(allowed, s, -1e30) for s in scores]
            exps = [
                jnp.exp2((s - jnp.max(s, axis=0, keepdims=True)) * (scale * math.log2(math.e))) for s in scores
            ]
            probs = [e * (1.0 / jnp.sum(e, axis=0, keepdims=True)) for e in exps]
            dscore = [
                (p * (d - jnp.sum(p * d, axis=0, keepdims=True))).astype(jnp.bfloat16)
                for p, d in zip(probs, dprob)
            ]
            for at, ds, q, k in zip(ats, dscore, q_rot, k_rot):
                grad_ref[0, rows, at] = unrope(lax.dot_general(ds, k, COLS, preferred_element_type=jnp.float32))
                grad_ref[1, rows, at] = unrope(jnp.dot(ds, q, preferred_element_type=jnp.float32))
    fetch.wait()


def attention_grads(query, key, value, grad, docs, weight, near):
    tokens, width = query.shape
    micro = tokens // SEQ
    return pl.pallas_call(
        attention_kernel,
        in_specs=[FAR] * 7,
        out_specs=[NEAR, NEAR],
        out_shape=[
            pltpu.VMEM((2, tokens, width), jnp.bfloat16),
            pltpu.VMEM((near, *weight.shape[1:]), jnp.bfloat16),
        ],
        scratch_shapes=[
            pltpu.VMEM((micro, 1, SEQ), jnp.int32),
            pltpu.VMEM((2, SEQ, HD), jnp.float32),
            pltpu.VMEM((4, tokens, width), jnp.bfloat16),
            pltpu.SemaphoreType.DMA((2,)),
            pltpu.SemaphoreType.DMA((micro, 4)),
            pltpu.SemaphoreType.DMA(()),
        ],
        cost_estimate=BRIEF,
        compiler_params=params(20),
        name="attention_grads",
    )(
        *(in_hbm(a) for a in (docs.reshape(micro, 1, SEQ), jnp.asarray(rope_tables()), query, key, value, grad, weight))
    )


def partials_kernel(pieces, grad_ref, near_ref, w_ref, out_ref, w_s, w_sem):
    owners, blocks, own_tokens, columns = out_ref.shape
    width = w_ref.shape[2]
    near = near_ref.shape[0] // columns
    depth = columns // pieces
    fetches = []
    for c in range((blocks - near) * pieces):
        source = w_ref.at[pl.ds(near * columns + c * depth, depth)]
        fetches.append(pltpu.make_async_copy(source, w_s.at[pl.ds(c * depth, depth)], w_sem.at[c]))
    for copy in fetches:
        copy.start()
    for start, ref in ((0, near_ref), (near, w_s)):
        if start:
            for copy in fetches:
                copy.wait()
        count = ref.shape[0] // columns
        step = min(count, max(1, SPAN // columns))
        for block in range(0, count, step):
            span = min(step, count - block) * columns
            weights = ref[block * columns : block * columns + span].reshape(span, 2 * width)
            out = lax.dot_general(grad_ref[0], weights[:, :width], ROWS, preferred_element_type=jnp.float32)
            out = out + lax.dot_general(grad_ref[1], weights[:, width:], ROWS, preferred_element_type=jnp.float32)
            out = out.astype(jnp.bfloat16)
            for at in range(span // columns):
                rows = out[:, at * columns : (at + 1) * columns]
                out_ref[:, start + block + at] = rows.reshape(owners, own_tokens, columns)


def input_partials(grads, near, weight, owners, blocks):
    _, tokens, width = grads.shape
    model = weight.shape[0]
    pieces = 2
    left = model - near.shape[0]
    return pl.pallas_call(
        functools.partial(partials_kernel, pieces),
        in_specs=[NEAR, NEAR, FAR],
        out_specs=NEAR,
        out_shape=pltpu.VMEM((owners, blocks, tokens // owners, model // blocks), jnp.bfloat16),
        scratch_shapes=[
            pltpu.VMEM((left, *weight.shape[1:]), jnp.bfloat16),
            pltpu.SemaphoreType.DMA((left * blocks * pieces // model,)),
        ],
        cost_estimate=BRIEF,
        compiler_params=params(36),
        name="input_partials",
    )(grads, near, in_hbm(weight))


def split_kernel(mirrors, x_ref, *refs):
    out_refs, sem = refs[:-1], refs[-1]
    data_count = len(out_refs)
    width = x_ref.shape[1] // (mirrors * data_count)
    copies = []
    for distance, out_ref in enumerate(out_refs):
        owner = lax.axis_index("dp") ^ distance
        for k in range(mirrors):
            block = lax.rem(lax.axis_index("mirror") + k, mirrors) * data_count + owner
            source = x_ref.at[:, pl.ds(pl.multiple_of(block * width, width), width)]
            target = out_ref.at[:, pl.ds(k * width, width)]
            copies.append(pltpu.make_async_copy(source, target, sem.at[distance, k]))
    for copy in copies:
        copy.start()
    for copy in copies:
        copy.wait()


def split_columns(rows, mirrors, data_count):
    tokens, model = rows.shape
    out = jax.ShapeDtypeStruct((tokens, model // data_count), rows.dtype)
    return pl.pallas_call(
        functools.partial(split_kernel, mirrors),
        in_specs=[FAR],
        out_specs=[FAR] * data_count,
        out_shape=[out] * data_count,
        scratch_shapes=[pltpu.SemaphoreType.DMA((data_count, mirrors))],
        cost_estimate=BRIEF,
        compiler_params=params(16),
        name="split_columns",
    )(in_hbm(rows))


def merge_kernel(*refs):
    in_refs, out_ref = refs[:-1], refs[-1]
    tokens = in_refs[0].shape[0]
    for i, in_ref in enumerate(in_refs):
        out_ref[i * tokens : (i + 1) * tokens, :] = in_ref[...]


def merge_tokens(columns):
    tokens, width = columns[0].shape
    return pl.pallas_call(
        merge_kernel,
        in_specs=[NEAR] * len(columns),
        out_specs=NEAR,
        out_shape=jax.ShapeDtypeStruct((len(columns) * tokens, width), columns[0].dtype),
        cost_estimate=BRIEF,
        compiler_params=params(16),
        name="merge_tokens",
    )(*columns)


def hop(values, parity, size, mirrors):
    pairs = []
    for i in range(size):
        j = i + 1 if i % 2 == parity else i - 1
        for r in range(mirrors):
            to = (j, r) if 0 <= j < size else (i, (r + 1) % mirrors)
            pairs.append((i * mirrors + r, to[0] * mirrors + to[1]))
    return lax.ppermute(values, ("tensor", "mirror"), pairs)


def has_partner(me, parity, size):
    ahead = lax.rem(me, 2) == parity
    partner = jnp.where(ahead, me + 1, me - 1)
    return (partner >= 0) & (partner < size), ahead


def pass_kernel(parity, distance, flow_ref, part_ref, out_ref):
    size = part_ref.shape[0]
    me = lax.axis_index("tensor")
    ahead = lax.rem(me, 2) == parity
    owner = jnp.where(ahead, me + distance, me - distance)
    active = (owner >= 0) & (owner < size)
    flows, _ = has_partner(me, 1 - parity, size)
    owner = jnp.clip(owner, 0, size - 1)

    @pl.when(flows & active)
    def _():
        out_ref[...] = flow_ref[...] + part_ref[owner]

    @pl.when(jnp.logical_not(flows))
    def _():
        out_ref[...] = part_ref[owner]

    @pl.when(flows & jnp.logical_not(active))
    def _():
        out_ref[...] = flow_ref[...]


def pass_on(flow, partials, parity, distance):
    return pl.pallas_call(
        functools.partial(pass_kernel, parity, distance),
        in_specs=[NEAR, NEAR],
        out_specs=NEAR,
        out_shape=jax.ShapeDtypeStruct(flow.shape, flow.dtype),
        cost_estimate=BRIEF,
        compiler_params=params(16),
        name="pass_on",
    )(flow, partials)


def finish_kernel(blocks, even_ref, odd_ref, part_ref, out_ref):
    size = part_ref.shape[0]
    me = lax.axis_index("tensor")
    tokens, columns = out_ref.shape[0], out_ref.shape[1] // blocks

    def store(total):
        for block in range(blocks):
            rows = total[block * tokens : (block + 1) * tokens]
            out_ref[:, block * columns : (block + 1) * columns] = rows.astype(out_ref.dtype)

    for parity, (flow_ref, other_ref) in enumerate(((odd_ref, even_ref), (even_ref, odd_ref))):
        alone = jnp.logical_not(has_partner(me, 1 - parity, size)[0])

        @pl.when(alone)
        def _(other_ref=other_ref):
            store(part_ref[me].astype(jnp.float32) + other_ref[...].astype(jnp.float32))

    both = has_partner(me, 0, size)[0] & has_partner(me, 1, size)[0]

    @pl.when(both)
    def _():
        total = part_ref[me].astype(jnp.float32) + even_ref[...].astype(jnp.float32)
        store(total + odd_ref[...].astype(jnp.float32))


def finish(even, odd, partials, blocks):
    rows, columns = even.shape
    return pl.pallas_call(
        functools.partial(finish_kernel, blocks),
        in_specs=[NEAR, NEAR, NEAR],
        out_specs=NEAR,
        out_shape=jax.ShapeDtypeStruct((rows // blocks, columns * blocks), even.dtype),
        cost_estimate=BRIEF,
        compiler_params=params(16),
        name="finish_input_grad",
    )(even, odd, partials)


def weight_kernel(counts, places, *refs):
    size, data_count, side, away = counts
    pieces = 2 * size - 1
    piece_refs, grad_refs = refs[:pieces], refs[pieces:-5]
    out_ref, x_s, grad_s, x_sem, grad_sem = refs[-5:]
    own_ref, even_refs, odd_refs = piece_refs[0], piece_refs[1 : size], piece_refs[size:]
    me = lax.axis_index("tensor")
    tokens = x_s.shape[0] // data_count
    own_tokens = tokens // size
    rows, width = x_s.shape[1], grad_s.shape[2]

    def fetch(ref, slot, k):
        owner = lax.rem(me - slot + size, size)
        start = pl.multiple_of(k * tokens + owner * own_tokens, own_tokens)
        source = ref.at[pl.ds(k * own_tokens, own_tokens), pl.ds(side * rows, rows)]
        return pltpu.make_async_copy(source, x_s.at[pl.ds(start, own_tokens)], x_sem.at[slot, k])

    odd_place = lax.rem(me, 2) == 1
    for k in range(data_count):
        fetch(own_ref, 0, k).start()
    for slot in range(1, size):
        behind = me >= slot
        came = (
            (behind & odd_place, even_refs[slot - 1]),
            (behind & jnp.logical_not(odd_place), odd_refs[slot - 1]),
            (jnp.logical_not(behind) & odd_place, odd_refs[size - slot - 1]),
            (jnp.logical_not(behind) & jnp.logical_not(odd_place), even_refs[size - slot - 1]),
        )
        for condition, ref in came:

            @pl.when(condition)
            def _(ref=ref, slot=slot):
                for k in range(data_count):
                    fetch(ref, slot, k).start()

    loads = []
    for j in range(2):
        for k in range(data_count):
            which, half = places[k][j]
            source = grad_refs[which] if half is None else grad_refs[which].at[half]
            target = grad_s.at[j, pl.ds(k * tokens, tokens)]
            loads.append(pltpu.make_async_copy(source, target, grad_sem.at[j, k]))
    for copy in loads:
        copy.start()
    for slot in range(size):
        for k in range(data_count):
            fetch(own_ref, slot, k).wait()
    for j in range(2):
        for copy in loads[j * data_count : (j + 1) * data_count]:
            copy.wait()
        total = lax.dot_general(x_s[...], grad_s[j], COLS, preferred_element_type=jnp.float32)
        out_ref[:, j * width : (j + 1) * width] = total.astype(out_ref.dtype)


def weight_sums(own, even, odd, grads, mirrors, side, dtype):
    size, data_count = len(even) + 1, len(grads)
    rows = own.shape[1] // mirrors
    arrays, places = [], []
    for pair in grads:
        place = []
        for array, half in pair:
            if not any(array is a for a in arrays):
                arrays.append(array)
            place.append(([i for i, a in enumerate(arrays) if a is array][0], half))
        places.append(place)
    tokens, width = arrays[0].shape[-2:]
    pieces = [own] + even + odd
    return pl.pallas_call(
        functools.partial(weight_kernel, (size, data_count, side, mirrors), places),
        in_specs=[FAR] * (len(pieces) + len(arrays)),
        out_specs=NEAR,
        out_shape=jax.ShapeDtypeStruct((rows, 2 * width), dtype),
        scratch_shapes=[
            pltpu.VMEM((data_count * tokens, rows), jnp.bfloat16),
            pltpu.VMEM((2, data_count * tokens, width), jnp.bfloat16),
            pltpu.SemaphoreType.DMA((size, data_count)),
            pltpu.SemaphoreType.DMA((2, data_count)),
        ],
        cost_estimate=pl.CostEstimate(flops=32 << 30, bytes_accessed=1 << 23, transcendentals=0),
        compiler_params=params(32),
        name="weight_sums",
    )(*pieces, *arrays)


def average_kernel(replicas, own_ref, *refs):
    away_refs, out_ref = refs[:-1], refs[-1]
    total = own_ref[...]
    for away_ref in away_refs:
        total = total + away_ref[...].astype(jnp.float32)
    out_ref[...] = (total * (1.0 / replicas)).reshape(out_ref.shape)


def average(own, away, replicas):
    rows, columns = own.shape
    depth = min(rows, 128)
    block = pl.BlockSpec((depth, columns), lambda i: (i, 0))
    return pl.pallas_call(
        functools.partial(average_kernel, replicas),
        grid=(rows // depth,),
        in_specs=[block] * (1 + len(away)),
        out_specs=pl.BlockSpec((depth, 2, columns // 2), lambda i: (i, 0, 0)),
        out_shape=jax.ShapeDtypeStruct((rows, 2, columns // 2), jnp.float32),
        cost_estimate=BRIEF,
        compiler_params=params(32),
        name="average_weight_grad",
    )(own, *away)


def swap(values, distance, size):
    return lax.ppermute(values, "dp", [(i, i ^ distance) for i in range(size)])


def across(values, distance, size):
    return lax.ppermute(values, "mirror", [(i, (i + distance) % size) for i in range(size)])


def gathered(grads, size):
    bits = [1 << b for b in range(size.bit_length() - 1)]
    near = {bit: swap(grads, bit, size) for bit in bits}
    found = []
    for half, order in enumerate((bits, bits[1:] + bits[:1])):
        blocks = {0: (grads, half)}
        for bit in order:
            for distance, (array, part) in list(blocks.items()):
                if distance == 0:
                    blocks[bit] = (near[bit], half)
                else:
                    moved = array if part is None else array[part]
                    blocks[distance ^ bit] = (swap(moved, bit, size), None)
        found.append(blocks)
    return [(found[0][d], found[1][d]) for d in range(size)]


def shards(layer_input, qk_weight, query_proj, key_proj, value_proj, head_grad, doc_ids):
    size = lax.axis_size("tensor")
    mirrors = lax.axis_size("mirror")
    data_count = lax.axis_size("dp")

    columns = split_columns(layer_input[0], mirrors, data_count)
    columns = [columns[0]] + [swap(columns[d], d, data_count) for d in range(1, data_count)]
    near = (3 * data_count + 3) // 4 * (layer_input.shape[2] // data_count)
    grads, weight_rows = attention_grads(
        query_proj[0], key_proj[0], value_proj[0], head_grad[0], doc_ids[0], qk_weight, near
    )
    columns, grads = lax.optimization_barrier((columns, grads))
    piece = merge_tokens(columns)

    gathered_grads = gathered(grads, data_count)
    partials = input_partials(grads, weight_rows, qk_weight, size, data_count)
    partials = partials.reshape(size, *piece.shape)

    even, odd = [hop(piece, 0, size, mirrors)], [hop(piece, 1, size, mirrors)]
    for distance in range(size - 1, 0, -1):
        send_even = pass_on(odd[-1], partials, 0, distance)
        send_odd = pass_on(even[-1], partials, 1, distance)
        if distance == 1:
            send_even, send_odd, own_piece = lax.optimization_barrier((send_even, send_odd, piece))
        even.append(hop(send_even, 0, size, mirrors))
        odd.append(hop(send_odd, 1, size, mirrors))

    away = []
    for r in range(1, mirrors):
        sums = weight_sums(own_piece, even[:-1], odd[:-1], gathered_grads, mirrors, r, jnp.bfloat16)
        away.append(across(sums, r, mirrors))
    own = weight_sums(own_piece, even[:-1], odd[:-1], gathered_grads, mirrors, 0, jnp.float32)
    weight_grad = average(own, away, mirrors * data_count)
    last_even, last_odd, weight_grad = lax.optimization_barrier((even[-1], odd[-1], weight_grad))
    input_grad = finish(last_even, last_odd, partials, data_count)[None]
    return (input_grad, weight_grad)


def solution(mesh):
    in_specs = (
        P(("mirror", "dp"), "tensor", None),
        P(None, None, "tensor"),
        P(("mirror", "dp"), None, "tensor"),
        P(("mirror", "dp"), None, "tensor"),
        P(("mirror", "dp"), None, "tensor"),
        P(("mirror", "dp"), None, "tensor"),
        P(("mirror", "dp"), None),
    )
    out_specs = (P(("mirror", "dp"), "tensor", None), P(("mirror", "dp"), None, "tensor"))
    return jax.shard_map(shards, mesh=mesh, in_specs=in_specs, out_specs=out_specs, check_vma=False)
```

```python
import functools
import math

import jax
import jax.numpy as jnp
import numpy as np
from jax import lax
from jax.experimental import pallas as pl
from jax.experimental.pallas import tpu as pltpu
from jax.sharding import PartitionSpec as P

HD = 128
SEQ = 128
GROUP = 4
SPAN = 1024
MIB = 1 << 20
ROWS = (((1,), (1,)), ((), ()))
COLS = (((0,), (0,)), ((), ()))
LENGTHY = pl.CostEstimate(flops=32 << 30, bytes_accessed=1 << 23, transcendentals=0)
BRIEF = pl.CostEstimate(flops=1, bytes_accessed=1, transcendentals=0)
NEAR = pl.BlockSpec(memory_space=pltpu.VMEM)
FAR = pl.BlockSpec(memory_space=pl.ANY)


def params(mib):
    return pltpu.CompilerParams(vmem_limit_bytes=mib * MIB)


def in_hbm(array):
    return pltpu.with_memory_space_constraint(array, pltpu.HBM)


def rope_tables():
    half = HD // 2
    inverse = np.exp(-(np.float32(2.0) * np.arange(half, dtype=np.float32) / np.float32(HD)) * np.float32(math.log(10000.0)))
    angles = np.arange(SEQ, dtype=np.float32)[:, None] * inverse[None, :].astype(np.float32)
    cosine, sine = np.cos(angles), np.sin(angles)
    return np.stack([np.concatenate([cosine, cosine], axis=1), np.concatenate([-sine, sine], axis=1)])


def attention_kernel(doc_ref, table_ref, q_ref, k_ref, v_ref, h_ref, w_ref, grad_ref, near_ref, doc_s, table_s, in_s, doc_sem, in_sem, w_sem):
    tokens, width = q_ref.shape
    scale = 1.0 / math.sqrt(HD)
    loads = []
    for b in range(tokens // SEQ):
        at = pl.ds(b * SEQ, SEQ)
        refs = enumerate((q_ref, k_ref, v_ref, h_ref))
        loads.append([pltpu.make_async_copy(ref.at[at], in_s.at[i, at], in_sem.at[b, i]) for i, ref in refs])
    first = [pltpu.make_async_copy(doc_ref, doc_s, doc_sem.at[0]), pltpu.make_async_copy(table_ref, table_s, doc_sem.at[1])]
    fetch = pltpu.make_async_copy(w_ref.at[pl.ds(0, near_ref.shape[0])], near_ref, w_sem)
    for copy in first + [c for load in loads for c in load] + [fetch]:
        copy.start()
    for copy in first:
        copy.wait()

    cosine, sine = table_s[0], table_s[1]
    back_cosine, back_sine = cosine * scale, sine * scale
    row = lax.broadcasted_iota(jnp.int32, (SEQ, SEQ), 0)
    col = lax.broadcasted_iota(jnp.int32, (SEQ, SEQ), 1)

    def rope(values):
        values = values.astype(jnp.float32)
        return (values * cosine + pltpu.roll(values, HD // 2, 1) * sine).astype(jnp.bfloat16)

    def unrope(values):
        return (values * back_cosine - pltpu.roll(values, HD // 2, 1) * back_sine).astype(jnp.bfloat16)

    for b in range(tokens // SEQ):
        rows = slice(b * SEQ, (b + 1) * SEQ)
        queries = lax.broadcast_in_dim(doc_s[b], (SEQ, SEQ), (0, 1))
        allowed = (row <= col) & (queries == queries.T)
        for copy in loads[b]:
            copy.wait()
        for first in range(0, width // HD, GROUP):
            ats = [slice(h * HD, (h + 1) * HD) for h in range(first, min(first + GROUP, width // HD))]
            q_rot = [rope(in_s[0, rows, at]) for at in ats]
            k_rot = [rope(in_s[1, rows, at]) for at in ats]
            scores = [
                lax.dot_general(k, q, ROWS, preferred_element_type=jnp.float32) for q, k in zip(q_rot, k_rot)
            ]
            dprob = [
                lax.dot_general(in_s[2, rows, at], in_s[3, rows, at], ROWS, preferred_element_type=jnp.float32)
                for at in ats
            ]
            scores = [jnp.where(allowed, s, -1e30) for s in scores]
            exps = [
                jnp.exp2((s - jnp.max(s, axis=0, keepdims=True)) * (scale * math.log2(math.e))) for s in scores
            ]
            probs = [e * (1.0 / jnp.sum(e, axis=0, keepdims=True)) for e in exps]
            dscore = [
                (p * (d - jnp.sum(p * d, axis=0, keepdims=True))).astype(jnp.bfloat16)
                for p, d in zip(probs, dprob)
            ]
            for at, ds, q, k in zip(ats, dscore, q_rot, k_rot):
                grad_ref[0, rows, at] = unrope(lax.dot_general(ds, k, COLS, preferred_element_type=jnp.float32))
                grad_ref[1, rows, at] = unrope(jnp.dot(ds, q, preferred_element_type=jnp.float32))
    fetch.wait()


def attention_grads(query, key, value, grad, docs, weight, near):
    tokens, width = query.shape
    micro = tokens // SEQ
    return pl.pallas_call(
        attention_kernel,
        in_specs=[FAR] * 7,
        out_specs=[NEAR, NEAR],
        out_shape=[
            pltpu.VMEM((2, tokens, width), jnp.bfloat16),
            pltpu.VMEM((near, *weight.shape[1:]), jnp.bfloat16),
        ],
        scratch_shapes=[
            pltpu.VMEM((micro, 1, SEQ), jnp.int32),
            pltpu.VMEM((2, SEQ, HD), jnp.float32),
            pltpu.VMEM((4, tokens, width), jnp.bfloat16),
            pltpu.SemaphoreType.DMA((2,)),
            pltpu.SemaphoreType.DMA((micro, 4)),
            pltpu.SemaphoreType.DMA(()),
        ],
        cost_estimate=BRIEF,
        compiler_params=params(20),
        name="attention_grads",
    )(
        *(in_hbm(a) for a in (docs.reshape(micro, 1, SEQ), jnp.asarray(rope_tables()), query, key, value, grad, weight))
    )


def partials_kernel(pieces, grad_ref, near_ref, w_ref, out_ref, w_s, w_sem):
    owners, blocks, own_tokens, columns = out_ref.shape
    width = w_ref.shape[2]
    near = near_ref.shape[0] // columns
    depth = columns // pieces
    fetches = []
    for c in range((blocks - near) * pieces):
        source = w_ref.at[pl.ds(near * columns + c * depth, depth)]
        fetches.append(pltpu.make_async_copy(source, w_s.at[pl.ds(c * depth, depth)], w_sem.at[c]))
    for copy in fetches:
        copy.start()
    for start, ref in ((0, near_ref), (near, w_s)):
        if start:
            for copy in fetches:
                copy.wait()
        count = ref.shape[0] // columns
        step = min(count, max(1, SPAN // columns))
        for block in range(0, count, step):
            span = min(step, count - block) * columns
            weights = ref[block * columns : block * columns + span].reshape(span, 2 * width)
            out = lax.dot_general(grad_ref[0], weights[:, :width], ROWS, preferred_element_type=jnp.float32)
            out = out + lax.dot_general(grad_ref[1], weights[:, width:], ROWS, preferred_element_type=jnp.float32)
            out = out.astype(jnp.bfloat16)
            for at in range(span // columns):
                rows = out[:, at * columns : (at + 1) * columns]
                out_ref[:, start + block + at] = rows.reshape(owners, own_tokens, columns)


def input_partials(grads, near, weight, owners, blocks):
    _, tokens, width = grads.shape
    model = weight.shape[0]
    pieces = 2
    left = model - near.shape[0]
    return pl.pallas_call(
        functools.partial(partials_kernel, pieces),
        in_specs=[NEAR, NEAR, FAR],
        out_specs=NEAR,
        out_shape=pltpu.VMEM((owners, blocks, tokens // owners, model // blocks), jnp.bfloat16),
        scratch_shapes=[
            pltpu.VMEM((left, *weight.shape[1:]), jnp.bfloat16),
            pltpu.SemaphoreType.DMA((left * blocks * pieces // model,)),
        ],
        cost_estimate=BRIEF,
        compiler_params=params(36),
        name="input_partials",
    )(grads, near, in_hbm(weight))


def split_kernel(mirrors, x_ref, *refs):
    out_refs, sem = refs[:-1], refs[-1]
    data_count = len(out_refs)
    width = x_ref.shape[1] // (mirrors * data_count)
    copies = []
    for distance, out_ref in enumerate(out_refs):
        owner = lax.axis_index("dp") ^ distance
        for k in range(mirrors):
            block = lax.rem(lax.axis_index("mirror") + k, mirrors) * data_count + owner
            source = x_ref.at[:, pl.ds(pl.multiple_of(block * width, width), width)]
            target = out_ref.at[:, pl.ds(k * width, width)]
            copies.append(pltpu.make_async_copy(source, target, sem.at[distance, k]))
    for copy in copies:
        copy.start()
    for copy in copies:
        copy.wait()


def split_columns(rows, mirrors, data_count):
    tokens, model = rows.shape
    out = jax.ShapeDtypeStruct((tokens, model // data_count), rows.dtype)
    return pl.pallas_call(
        functools.partial(split_kernel, mirrors),
        in_specs=[FAR],
        out_specs=[FAR] * data_count,
        out_shape=[out] * data_count,
        scratch_shapes=[pltpu.SemaphoreType.DMA((data_count, mirrors))],
        cost_estimate=BRIEF,
        compiler_params=params(16),
        name="split_columns",
    )(in_hbm(rows))


def merge_kernel(*refs):
    in_refs, out_ref = refs[:-1], refs[-1]
    tokens = in_refs[0].shape[0]
    for i, in_ref in enumerate(in_refs):
        out_ref[i * tokens : (i + 1) * tokens, :] = in_ref[...]


def merge_tokens(columns):
    tokens, width = columns[0].shape
    return pl.pallas_call(
        merge_kernel,
        in_specs=[NEAR] * len(columns),
        out_specs=NEAR,
        out_shape=jax.ShapeDtypeStruct((len(columns) * tokens, width), columns[0].dtype),
        cost_estimate=BRIEF,
        compiler_params=params(16),
        name="merge_tokens",
    )(*columns)


def hop(values, parity, size, mirrors):
    pairs = []
    for i in range(size):
        j = i + 1 if i % 2 == parity else i - 1
        for r in range(mirrors):
            to = (j, r) if 0 <= j < size else (i, (r + 1) % mirrors)
            pairs.append((i * mirrors + r, to[0] * mirrors + to[1]))
    return lax.ppermute(values, ("tensor", "mirror"), pairs)


def has_partner(me, parity, size):
    ahead = lax.rem(me, 2) == parity
    partner = jnp.where(ahead, me + 1, me - 1)
    return (partner >= 0) & (partner < size), ahead


def pass_kernel(parity, distance, flow_ref, part_ref, out_ref):
    size = part_ref.shape[0]
    me = lax.axis_index("tensor")
    ahead = lax.rem(me, 2) == parity
    owner = jnp.where(ahead, me + distance, me - distance)
    active = (owner >= 0) & (owner < size)
    flows, _ = has_partner(me, 1 - parity, size)
    owner = jnp.clip(owner, 0, size - 1)

    @pl.when(flows & active)
    def _():
        out_ref[...] = flow_ref[...] + part_ref[owner]

    @pl.when(jnp.logical_not(flows))
    def _():
        out_ref[...] = part_ref[owner]

    @pl.when(flows & jnp.logical_not(active))
    def _():
        out_ref[...] = flow_ref[...]


def pass_on(flow, partials, parity, distance):
    return pl.pallas_call(
        functools.partial(pass_kernel, parity, distance),
        in_specs=[NEAR, NEAR],
        out_specs=NEAR,
        out_shape=jax.ShapeDtypeStruct(flow.shape, flow.dtype),
        cost_estimate=BRIEF,
        compiler_params=params(16),
        name="pass_on",
    )(flow, partials)


def finish_kernel(blocks, even_ref, odd_ref, part_ref, out_ref):
    size = part_ref.shape[0]
    me = lax.axis_index("tensor")
    tokens, columns = out_ref.shape[0], out_ref.shape[1] // blocks

    def store(total):
        for block in range(blocks):
            rows = total[block * tokens : (block + 1) * tokens]
            out_ref[:, block * columns : (block + 1) * columns] = rows.astype(out_ref.dtype)

    for parity, (flow_ref, other_ref) in enumerate(((odd_ref, even_ref), (even_ref, odd_ref))):
        alone = jnp.logical_not(has_partner(me, 1 - parity, size)[0])

        @pl.when(alone)
        def _(other_ref=other_ref):
            store(part_ref[me].astype(jnp.float32) + other_ref[...].astype(jnp.float32))

    both = has_partner(me, 0, size)[0] & has_partner(me, 1, size)[0]

    @pl.when(both)
    def _():
        total = part_ref[me].astype(jnp.float32) + even_ref[...].astype(jnp.float32)
        store(total + odd_ref[...].astype(jnp.float32))


def finish(even, odd, partials, blocks):
    rows, columns = even.shape
    return pl.pallas_call(
        functools.partial(finish_kernel, blocks),
        in_specs=[NEAR, NEAR, NEAR],
        out_specs=NEAR,
        out_shape=jax.ShapeDtypeStruct((rows // blocks, columns * blocks), even.dtype),
        cost_estimate=BRIEF,
        compiler_params=params(16),
        name="finish_input_grad",
    )(even, odd, partials)


def piece_cases(me, size, even_refs, odd_refs):
    odd_place = lax.rem(me, 2) == 1
    even_place = jnp.logical_not(odd_place)
    cases = []
    for slot in range(1, size):
        behind = me >= slot
        beyond = jnp.logical_not(behind)
        back = size - slot
        cases.append(
            (
                (behind & odd_place, even_refs, slot),
                (behind & even_place, odd_refs, slot),
                (beyond & odd_place, odd_refs, back),
                (beyond & even_place, even_refs, back),
            )
        )
    return [[(c, refs[hop - 1] if hop <= len(refs) else None, hop == size - 1) for c, refs, hop in case] for case in cases]


def early_kernel(size, side, places, *refs):
    out_ref, x_s = refs[-2:]
    hops = size - 2
    own_ref, even_refs, odd_refs = refs[0], refs[1 : 1 + hops], refs[1 + hops : 1 + 2 * hops]
    grad_refs = views(refs[1 + 2 * hops : -2], places)
    count = len(grad_refs) // 2
    me = lax.axis_index("tensor")
    tokens, rows = x_s.shape[1:]
    own_tokens = tokens // size
    width = out_ref.shape[1] // 2

    def place(ref, slot):
        start = pl.multiple_of(lax.rem(me - slot + size, size) * own_tokens, own_tokens)
        for k in range(count):
            if ref is None:
                values = jnp.zeros((own_tokens, rows), x_s.dtype)
            else:
                values = ref[k * own_tokens : (k + 1) * own_tokens, side * rows : (side + 1) * rows]
            x_s[k, pl.ds(start, own_tokens), :] = values

    place(own_ref, 0)
    for slot, case in enumerate(piece_cases(me, size, even_refs, odd_refs), 1):
        for condition, ref, _ in case:

            @pl.when(condition)
            def _(ref=ref, slot=slot):
                place(ref, slot)

    turned = [x_s[k].T for k in range(count)]
    for j in range(2):
        total = None
        for k in range(count):
            term = jnp.dot(turned[k], grad_refs[j * count + k][...], preferred_element_type=jnp.float32)
            total = term if total is None else total + term
        out_ref[:, j * width : (j + 1) * width] = total


def late_kernel(size, side, places, *refs):
    sum_ref, refs = refs[0], refs[1:]
    out_ref, x_s, last_s, grad_s = refs[-4:]
    hops = size - 1
    own_ref, even_refs, odd_refs = refs[0], refs[1 : 1 + hops], refs[1 + hops : 1 + 2 * hops]
    grad_refs = views(refs[1 + 2 * hops : -4], places)
    count = len(grad_refs) // 2
    me = lax.axis_index("tensor")
    tokens, rows = x_s.shape
    own_tokens = tokens // size
    width = out_ref.shape[1] // 2
    columns = slice(side * rows, (side + 1) * rows)
    far = slice((count - 1) * own_tokens, count * own_tokens)

    def place(ref, slot):
        start = pl.multiple_of(lax.rem(me - slot + size, size) * own_tokens, own_tokens)
        x_s[pl.ds(start, own_tokens), :] = ref[far, columns]

    place(own_ref, 0)
    last_s[...] = jnp.zeros_like(last_s)
    for slot, case in enumerate(piece_cases(me, size, even_refs, odd_refs), 1):
        for condition, ref, last in case:

            @pl.when(condition)
            def _(ref=ref, slot=slot, last=last):
                place(ref, slot)
                if last:
                    last_s[...] = ref[: last_s.shape[0], columns]

    owner = jnp.where(me == 0, size - 1, 0)
    start = pl.multiple_of(owner * own_tokens, own_tokens)
    for j in range(2):
        for k in range(count - 1):
            grad_s[j, k * own_tokens : (k + 1) * own_tokens, :] = grad_refs[j * count + k][pl.ds(start, own_tokens), :]
    turned, last_turned = x_s[...].T, last_s[...].T
    for j in range(2):
        at = slice(j * width, (j + 1) * width)
        total = jnp.dot(turned, grad_refs[j * count + count - 1][...], preferred_element_type=jnp.float32)
        total = total + jnp.dot(last_turned, grad_s[j], preferred_element_type=jnp.float32)
        out_ref[:, at] = (sum_ref[:, at] + total).astype(out_ref.dtype)


def views(refs, places):
    return [refs[which] if half is None else refs[which].at[half] for which, half in places]


def grad_operands(grads):
    arrays, places = [], []
    for array, half in grads:
        if not any(array is a for a in arrays):
            arrays.append(array)
        places.append(([i for i, a in enumerate(arrays) if a is array][0], half))
    return arrays, places


def early_sums(own, even, odd, grads, mirrors, side, size):
    rows = own.shape[1] // mirrors
    grads, places = grad_operands([g for half in grads for g in half[:-1]])
    tokens, width = grads[0].shape[-2:]
    pieces = [own, *even, *odd]
    return pl.pallas_call(
        functools.partial(early_kernel, size, side, places),
        in_specs=[NEAR] * (len(pieces) + len(grads)),
        out_specs=NEAR,
        out_shape=jax.ShapeDtypeStruct((rows, 2 * width), jnp.float32),
        scratch_shapes=[pltpu.VMEM((len(places) // 2, tokens, rows), jnp.bfloat16)],
        cost_estimate=LENGTHY,
        compiler_params=params(24),
        name="early_sums",
    )(*pieces, *grads)


def late_sums(sums, own, even, odd, grads, mirrors, side, size, dtype):
    rows = own.shape[1] // mirrors
    grads, places = grad_operands([g for half in grads for g in half])
    tokens, width = grads[0].shape[-2:]
    pieces = [sums, own, *even, *odd]
    last = (len(places) // 2 - 1) * (tokens // size)
    return pl.pallas_call(
        functools.partial(late_kernel, size, side, places),
        in_specs=[NEAR] * (len(pieces) + len(grads)),
        out_specs=NEAR,
        out_shape=jax.ShapeDtypeStruct((rows, 2 * width), dtype),
        scratch_shapes=[
            pltpu.VMEM((tokens, rows), jnp.bfloat16),
            pltpu.VMEM((last, rows), jnp.bfloat16),
            pltpu.VMEM((2, last, width), jnp.bfloat16),
        ],
        cost_estimate=LENGTHY,
        compiler_params=params(24),
        name="late_sums",
    )(*pieces, *grads)


def average_kernel(replicas, own_ref, *refs):
    away_refs, out_ref = refs[:-1], refs[-1]
    total = own_ref[...]
    for away_ref in away_refs:
        total = total + away_ref[...].astype(jnp.float32)
    out_ref[...] = (total * (1.0 / replicas)).reshape(out_ref.shape)


def average(own, away, replicas):
    rows, columns = own.shape
    depth = min(rows, 128)
    block = pl.BlockSpec((depth, columns), lambda i: (i, 0))
    return pl.pallas_call(
        functools.partial(average_kernel, replicas),
        grid=(rows // depth,),
        in_specs=[block] * (1 + len(away)),
        out_specs=pl.BlockSpec((depth, 2, columns // 2), lambda i: (i, 0, 0)),
        out_shape=jax.ShapeDtypeStruct((rows, 2, columns // 2), jnp.float32),
        cost_estimate=BRIEF,
        compiler_params=params(32),
        name="average_weight_grad",
    )(own, *away)


def swap(values, distance, size):
    return lax.ppermute(values, "dp", [(i, i ^ distance) for i in range(size)])


def across(values, distance, size):
    return lax.ppermute(values, "mirror", [(i, (i + distance) % size) for i in range(size)])


def gathered(grads, size):
    bits = [1 << b for b in range(size.bit_length() - 1)]
    near = {bit: swap(grads, bit, size) for bit in bits}
    found = []
    for half, order in enumerate((bits, bits[1:] + bits[:1])):
        blocks = {0: (grads, half)}
        for bit in order:
            for distance, (array, part) in list(blocks.items()):
                if distance == 0:
                    blocks[bit] = (near[bit], half)
                else:
                    moved = array if part is None else array[part]
                    blocks[distance ^ bit] = (swap(moved, bit, size), None)
        found.append([blocks[d] for d in range(size)])
    return found


def shards(layer_input, qk_weight, query_proj, key_proj, value_proj, head_grad, doc_ids):
    size = lax.axis_size("tensor")
    mirrors = lax.axis_size("mirror")
    data_count = lax.axis_size("dp")

    columns = split_columns(layer_input[0], mirrors, data_count)
    columns = [columns[0]] + [swap(columns[d], d, data_count) for d in range(1, data_count)]
    near = (3 * data_count + 3) // 4 * (layer_input.shape[2] // data_count)
    grads, weight_rows = attention_grads(
        query_proj[0], key_proj[0], value_proj[0], head_grad[0], doc_ids[0], qk_weight, near
    )
    columns, grads = lax.optimization_barrier((columns, grads))
    piece = merge_tokens(columns)
    partials = input_partials(grads, weight_rows, qk_weight, size, data_count)
    partials = partials.reshape(size, *piece.shape)

    even, odd = [hop(piece, 0, size, mirrors)], [hop(piece, 1, size, mirrors)]
    for distance in range(size - 1, 0, -1):
        send_even = pass_on(odd[-1], partials, 0, distance)
        send_odd = pass_on(even[-1], partials, 1, distance)
        if distance == 1:
            send_even, send_odd, own_piece = lax.optimization_barrier((send_even, send_odd, piece))
        even.append(hop(send_even, 0, size, mirrors))
        odd.append(hop(send_odd, 1, size, mirrors))

    grads = gathered(grads, data_count)
    sides = range(mirrors)
    early = [early_sums(piece, even[:-2], odd[:-2], grads, mirrors, side, size) for side in sides]
    away = []
    for side in sides[1:]:
        sums = late_sums(early[side], own_piece, even[:-1], odd[:-1], grads, mirrors, side, size, jnp.bfloat16)
        away.append(across(sums, side, mirrors))
    own = late_sums(early[0], own_piece, even[:-1], odd[:-1], grads, mirrors, 0, size, jnp.float32)
    weight_grad = average(own, away, mirrors * data_count)
    last_even, last_odd, weight_grad = lax.optimization_barrier((even[-1], odd[-1], weight_grad))
    input_grad = finish(last_even, last_odd, partials, data_count)[None]
    return (input_grad, weight_grad)


def solution(mesh):
    in_specs = (
        P(("mirror", "dp"), "tensor", None),
        P(None, None, "tensor"),
        P(("mirror", "dp"), None, "tensor"),
        P(("mirror", "dp"), None, "tensor"),
        P(("mirror", "dp"), None, "tensor"),
        P(("mirror", "dp"), None, "tensor"),
        P(("mirror", "dp"), None),
    )
    out_specs = (P(("mirror", "dp"), "tensor", None), P(("mirror", "dp"), None, "tensor"))
    return jax.shard_map(shards, mesh=mesh, in_specs=in_specs, out_specs=out_specs, check_vma=False)
```

```python
import functools
import math

import jax
import jax.numpy as jnp
import numpy as np
from jax import lax
from jax.experimental import pallas as pl
from jax.experimental.pallas import tpu as pltpu
from jax.sharding import PartitionSpec as P

HD = 128
SEQ = 128
GROUP = 4
SPAN = 1024
PARTS = 1
MIB = 1 << 20
ROWS = (((1,), (1,)), ((), ()))
COLS = (((0,), (0,)), ((), ()))
LENGTHY = pl.CostEstimate(flops=32 << 30, bytes_accessed=1 << 23, transcendentals=0)
BRIEF = pl.CostEstimate(flops=1, bytes_accessed=1, transcendentals=0)
NEAR = pl.BlockSpec(memory_space=pltpu.VMEM)
FAR = pl.BlockSpec(memory_space=pl.ANY)


def params(mib):
    return pltpu.CompilerParams(vmem_limit_bytes=mib * MIB)


def in_hbm(array):
    return pltpu.with_memory_space_constraint(array, pltpu.HBM)


def rope_tables():
    half = HD // 2
    inverse = np.exp(-(np.float32(2.0) * np.arange(half, dtype=np.float32) / np.float32(HD)) * np.float32(math.log(10000.0)))
    angles = np.arange(SEQ, dtype=np.float32)[:, None] * inverse[None, :].astype(np.float32)
    cosine, sine = np.cos(angles), np.sin(angles)
    return np.stack([np.concatenate([cosine, cosine], axis=1), np.concatenate([-sine, sine], axis=1)])


def attention_kernel(doc_ref, table_ref, q_ref, k_ref, v_ref, h_ref, w_ref, grad_ref, near_ref, doc_s, table_s, in_s, doc_sem, in_sem, w_sem):
    tokens, width = q_ref.shape
    scale = 1.0 / math.sqrt(HD)
    loads = []
    for b in range(tokens // SEQ):
        at = pl.ds(b * SEQ, SEQ)
        refs = enumerate((q_ref, k_ref, v_ref, h_ref))
        loads.append([pltpu.make_async_copy(ref.at[at], in_s.at[i, at], in_sem.at[b, i]) for i, ref in refs])
    first = [pltpu.make_async_copy(doc_ref, doc_s, doc_sem.at[0]), pltpu.make_async_copy(table_ref, table_s, doc_sem.at[1])]
    fetch = pltpu.make_async_copy(w_ref.at[pl.ds(0, near_ref.shape[0])], near_ref, w_sem)
    for copy in first + [c for load in loads for c in load] + [fetch]:
        copy.start()
    for copy in first:
        copy.wait()

    cosine, sine = table_s[0], table_s[1]
    back_cosine, back_sine = cosine * scale, sine * scale
    row = lax.broadcasted_iota(jnp.int32, (SEQ, SEQ), 0)
    col = lax.broadcasted_iota(jnp.int32, (SEQ, SEQ), 1)

    def rope(values):
        values = values.astype(jnp.float32)
        return (values * cosine + pltpu.roll(values, HD // 2, 1) * sine).astype(jnp.bfloat16)

    def unrope(values):
        return (values * back_cosine - pltpu.roll(values, HD // 2, 1) * back_sine).astype(jnp.bfloat16)

    for b in range(tokens // SEQ):
        rows = slice(b * SEQ, (b + 1) * SEQ)
        queries = lax.broadcast_in_dim(doc_s[b], (SEQ, SEQ), (0, 1))
        allowed = (row <= col) & (queries == queries.T)
        for copy in loads[b]:
            copy.wait()
        for first in range(0, width // HD, GROUP):
            ats = [slice(h * HD, (h + 1) * HD) for h in range(first, min(first + GROUP, width // HD))]
            q_rot = [rope(in_s[0, rows, at]) for at in ats]
            k_rot = [rope(in_s[1, rows, at]) for at in ats]
            scores = [
                lax.dot_general(k, q, ROWS, preferred_element_type=jnp.float32) for q, k in zip(q_rot, k_rot)
            ]
            dprob = [
                lax.dot_general(in_s[2, rows, at], in_s[3, rows, at], ROWS, preferred_element_type=jnp.float32)
                for at in ats
            ]
            scores = [jnp.where(allowed, s, -1e30) for s in scores]
            exps = [
                jnp.exp2((s - jnp.max(s, axis=0, keepdims=True)) * (scale * math.log2(math.e))) for s in scores
            ]
            probs = [e * (1.0 / jnp.sum(e, axis=0, keepdims=True)) for e in exps]
            dscore = [
                (p * (d - jnp.sum(p * d, axis=0, keepdims=True))).astype(jnp.bfloat16)
                for p, d in zip(probs, dprob)
            ]
            for at, ds, q, k in zip(ats, dscore, q_rot, k_rot):
                grad_ref[0, rows, at] = unrope(lax.dot_general(ds, k, COLS, preferred_element_type=jnp.float32))
                grad_ref[1, rows, at] = unrope(jnp.dot(ds, q, preferred_element_type=jnp.float32))
    fetch.wait()


def attention_grads(query, key, value, grad, docs, weight, near):
    tokens, width = query.shape
    micro = tokens // SEQ
    return pl.pallas_call(
        attention_kernel,
        in_specs=[FAR] * 7,
        out_specs=[NEAR, NEAR],
        out_shape=[
            pltpu.VMEM((2, tokens, width), jnp.bfloat16),
            pltpu.VMEM((near, *weight.shape[1:]), jnp.bfloat16),
        ],
        scratch_shapes=[
            pltpu.VMEM((micro, 1, SEQ), jnp.int32),
            pltpu.VMEM((2, SEQ, HD), jnp.float32),
            pltpu.VMEM((4, tokens, width), jnp.bfloat16),
            pltpu.SemaphoreType.DMA((2,)),
            pltpu.SemaphoreType.DMA((micro, 4)),
            pltpu.SemaphoreType.DMA(()),
        ],
        cost_estimate=BRIEF,
        compiler_params=params(20),
        name="attention_grads",
    )(
        *(in_hbm(a) for a in (docs.reshape(micro, 1, SEQ), jnp.asarray(rope_tables()), query, key, value, grad, weight))
    )


def partials_kernel(pieces, grad_ref, near_ref, w_ref, out_ref, w_s, w_sem):
    owners, blocks, own_tokens, columns = out_ref.shape
    width = w_ref.shape[2]
    near = near_ref.shape[0] // columns
    depth = columns // pieces
    fetches = []
    for c in range((blocks - near) * pieces):
        source = w_ref.at[pl.ds(near * columns + c * depth, depth)]
        fetches.append(pltpu.make_async_copy(source, w_s.at[pl.ds(c * depth, depth)], w_sem.at[c]))
    for copy in fetches:
        copy.start()
    for start, ref in ((0, near_ref), (near, w_s)):
        if start:
            for copy in fetches:
                copy.wait()
        count = ref.shape[0] // columns
        step = min(count, max(1, SPAN // columns))
        for block in range(0, count, step):
            span = min(step, count - block) * columns
            weights = ref[block * columns : block * columns + span].reshape(span, 2 * width)
            out = lax.dot_general(grad_ref[0], weights[:, :width], ROWS, preferred_element_type=jnp.float32)
            out = out + lax.dot_general(grad_ref[1], weights[:, width:], ROWS, preferred_element_type=jnp.float32)
            out = out.astype(jnp.bfloat16)
            for at in range(span // columns):
                rows = out[:, at * columns : (at + 1) * columns]
                out_ref[:, start + block + at] = rows.reshape(owners, own_tokens, columns)


def input_partials(grads, near, weight, owners, blocks):
    _, tokens, width = grads.shape
    model = weight.shape[0]
    pieces = 2
    left = model - near.shape[0]
    return pl.pallas_call(
        functools.partial(partials_kernel, pieces),
        in_specs=[NEAR, NEAR, FAR],
        out_specs=NEAR,
        out_shape=pltpu.VMEM((owners, blocks, tokens // owners, model // blocks), jnp.bfloat16),
        scratch_shapes=[
            pltpu.VMEM((left, *weight.shape[1:]), jnp.bfloat16),
            pltpu.SemaphoreType.DMA((left * blocks * pieces // model,)),
        ],
        cost_estimate=BRIEF,
        compiler_params=params(36),
        name="input_partials",
    )(grads, near, in_hbm(weight))


def split_kernel(mirrors, x_ref, *refs):
    out_refs, sem = refs[:-1], refs[-1]
    data_count = len(out_refs)
    width = x_ref.shape[1] // (mirrors * data_count)
    copies = []
    for distance, out_ref in enumerate(out_refs):
        owner = lax.axis_index("dp") ^ distance
        for k in range(mirrors):
            block = lax.rem(lax.axis_index("mirror") + k, mirrors) * data_count + owner
            source = x_ref.at[:, pl.ds(pl.multiple_of(block * width, width), width)]
            target = out_ref.at[:, pl.ds(k * width, width)]
            copies.append(pltpu.make_async_copy(source, target, sem.at[distance, k]))
    for copy in copies:
        copy.start()
    for copy in copies:
        copy.wait()


def split_columns(rows, mirrors, data_count):
    tokens, model = rows.shape
    out = jax.ShapeDtypeStruct((tokens, model // data_count), rows.dtype)
    return pl.pallas_call(
        functools.partial(split_kernel, mirrors),
        in_specs=[FAR],
        out_specs=[FAR] * data_count,
        out_shape=[out] * data_count,
        scratch_shapes=[pltpu.SemaphoreType.DMA((data_count, mirrors))],
        cost_estimate=BRIEF,
        compiler_params=params(16),
        name="split_columns",
    )(in_hbm(rows))


def merge_kernel(*refs):
    in_refs, out_ref = refs[:-1], refs[-1]
    tokens = in_refs[0].shape[0]
    for i, in_ref in enumerate(in_refs):
        out_ref[i * tokens : (i + 1) * tokens, :] = in_ref[...]


def merge_tokens(columns):
    tokens, width = columns[0].shape
    return pl.pallas_call(
        merge_kernel,
        in_specs=[NEAR] * len(columns),
        out_specs=NEAR,
        out_shape=jax.ShapeDtypeStruct((len(columns) * tokens, width), columns[0].dtype),
        cost_estimate=BRIEF,
        compiler_params=params(16),
        name="merge_tokens",
    )(*columns)


def hop(values, parity, size, mirrors):
    pairs = []
    for i in range(size):
        j = i + 1 if i % 2 == parity else i - 1
        for r in range(mirrors):
            to = (j, r) if 0 <= j < size else (i, (r + 1) % mirrors)
            pairs.append((i * mirrors + r, to[0] * mirrors + to[1]))
    return lax.ppermute(values, ("tensor", "mirror"), pairs)


def has_partner(me, parity, size):
    ahead = lax.rem(me, 2) == parity
    partner = jnp.where(ahead, me + 1, me - 1)
    return (partner >= 0) & (partner < size), ahead


def pass_kernel(parity, distance, part, flow_ref, partial_ref, out_ref):
    size = partial_ref.shape[0]
    me = lax.axis_index("tensor")
    ahead = lax.rem(me, 2) == parity
    owner = jnp.where(ahead, me + distance, me - distance)
    active = (owner >= 0) & (owner < size)
    flows, _ = has_partner(me, 1 - parity, size)
    owner = jnp.clip(owner, 0, size - 1)
    height = out_ref.shape[0]
    rows = slice(part * height, (part + 1) * height)
    flow_rows = rows if flow_ref.shape[0] > height else slice(0, height)

    @pl.when(flows & active)
    def _():
        out_ref[...] = flow_ref[flow_rows] + partial_ref[owner, rows]

    @pl.when(jnp.logical_not(flows))
    def _():
        out_ref[...] = partial_ref[owner, rows]

    @pl.when(flows & jnp.logical_not(active))
    def _():
        out_ref[...] = flow_ref[flow_rows]


def pass_on(flow, partials, parity, distance, part, parts):
    _, rows, columns = partials.shape
    return pl.pallas_call(
        functools.partial(pass_kernel, parity, distance, part),
        in_specs=[NEAR, NEAR],
        out_specs=NEAR,
        out_shape=jax.ShapeDtypeStruct((rows // parts, columns), partials.dtype),
        cost_estimate=BRIEF,
        compiler_params=params(16),
        name="pass_on",
    )(flow, partials)


def finish_kernel(blocks, parts, *refs):
    odd_refs, even_refs, (partial_ref, out_ref) = refs[:parts], refs[parts : 2 * parts], refs[2 * parts :]
    size = partial_ref.shape[0]
    me = lax.axis_index("tensor")
    tokens, columns = out_ref.shape[0], out_ref.shape[1] // blocks
    has_even, has_odd = (has_partner(me, parity, size)[0] for parity in range(2))

    def store(*flows):
        for block in range(blocks):
            per = blocks // parts
            rows = slice(block % per * tokens, (block % per + 1) * tokens)
            total = partial_ref[me, block * tokens : (block + 1) * tokens].astype(jnp.float32)
            for refs in flows:
                total = total + refs[block // per][rows].astype(jnp.float32)
            out_ref[:, block * columns : (block + 1) * columns] = total.astype(out_ref.dtype)

    @pl.when(has_even & has_odd)
    def _():
        store(even_refs, odd_refs)

    @pl.when(jnp.logical_not(has_odd))
    def _():
        store(even_refs)

    @pl.when(jnp.logical_not(has_even))
    def _():
        store(odd_refs)


def finish(even, odd, partials, blocks):
    _, rows, columns = partials.shape
    return pl.pallas_call(
        functools.partial(finish_kernel, blocks, len(even)),
        in_specs=[NEAR] * (2 * len(even) + 1),
        out_specs=NEAR,
        out_shape=jax.ShapeDtypeStruct((rows // blocks, columns * blocks), partials.dtype),
        cost_estimate=BRIEF,
        compiler_params=params(16),
        name="finish_input_grad",
    )(*odd, *even, partials)


def grouped(refs, counts):
    groups, at = [], 0
    for count in counts:
        groups.append(refs[at : at + count])
        at += count
    return groups


def replica_rows(parts, k, own_tokens):
    height = parts[0].shape[0]
    start = k * own_tokens % height
    return parts[k * own_tokens // height], slice(start, start + own_tokens)


def piece_cases(me, size, even_refs, odd_refs):
    odd_place = lax.rem(me, 2) == 1
    even_place = jnp.logical_not(odd_place)
    cases = []
    for slot in range(1, size):
        behind = me >= slot
        beyond = jnp.logical_not(behind)
        back = size - slot
        cases.append(
            (
                (behind & odd_place, even_refs, slot),
                (behind & even_place, odd_refs, slot),
                (beyond & odd_place, odd_refs, back),
                (beyond & even_place, even_refs, back),
            )
        )
    return [[(c, refs[hop - 1] if hop <= len(refs) else None, hop == size - 1) for c, refs, hop in case] for case in cases]


def early_kernel(size, side, counts, places, *refs):
    out_ref, x_s = refs[-2:]
    pieces = grouped(refs[: sum(counts)], counts)
    own_ref, odd_refs, even_refs = pieces[0], pieces[1 : size - 1], pieces[size - 1 :]
    grad_refs = views(refs[sum(counts) : -2], places)
    count = len(grad_refs) // 2
    me = lax.axis_index("tensor")
    tokens, rows = x_s.shape[1:]
    own_tokens = tokens // size
    width = out_ref.shape[1] // 2

    def place(ref, slot):
        start = pl.multiple_of(lax.rem(me - slot + size, size) * own_tokens, own_tokens)
        for k in range(count):
            if ref is None:
                values = jnp.zeros((own_tokens, rows), x_s.dtype)
            else:
                part, at = replica_rows(ref, k, own_tokens)
                values = part[at, side * rows : (side + 1) * rows]
            x_s[k, pl.ds(start, own_tokens), :] = values

    place(own_ref, 0)
    for slot, case in enumerate(piece_cases(me, size, even_refs, odd_refs), 1):
        for condition, ref, _ in case:

            @pl.when(condition)
            def _(ref=ref, slot=slot):
                place(ref, slot)

    turned = [x_s[k].T for k in range(count)]
    for j in range(2):
        total = None
        for k in range(count):
            term = jnp.dot(turned[k], grad_refs[j * count + k][...], preferred_element_type=jnp.float32)
            total = term if total is None else total + term
        out_ref[:, j * width : (j + 1) * width] = total


def late_kernel(size, side, counts, places, *refs):
    sum_ref, refs = refs[0], refs[1:]
    out_ref, x_s, last_s, grad_s = refs[-4:]
    pieces = grouped(refs[: sum(counts)], counts)
    own_ref, odd_refs, even_refs = pieces[0], pieces[1:size], pieces[size:]
    grad_refs = views(refs[sum(counts) : -4], places)
    count = len(grad_refs) // 2
    me = lax.axis_index("tensor")
    tokens, rows = x_s.shape
    own_tokens = tokens // size
    width = out_ref.shape[1] // 2
    columns = slice(side * rows, (side + 1) * rows)

    def place(ref, slot):
        start = pl.multiple_of(lax.rem(me - slot + size, size) * own_tokens, own_tokens)
        part, at = replica_rows(ref, count - 1, own_tokens)
        x_s[pl.ds(start, own_tokens), :] = part[at, columns]

    place(own_ref, 0)
    last_s[...] = jnp.zeros_like(last_s)
    for slot, case in enumerate(piece_cases(me, size, even_refs, odd_refs), 1):
        for condition, ref, last in case:

            @pl.when(condition)
            def _(ref=ref, slot=slot, last=last):
                place(ref, slot)
                if last:
                    for k in range(count - 1):
                        part, at = replica_rows(ref, k, own_tokens)
                        last_s[k * own_tokens : (k + 1) * own_tokens, :] = part[at, columns]

    owner = jnp.where(me == 0, size - 1, 0)
    start = pl.multiple_of(owner * own_tokens, own_tokens)
    for j in range(2):
        for k in range(count - 1):
            grad_s[j, k * own_tokens : (k + 1) * own_tokens, :] = grad_refs[j * count + k][pl.ds(start, own_tokens), :]
    turned, last_turned = x_s[...].T, last_s[...].T
    for j in range(2):
        at = slice(j * width, (j + 1) * width)
        total = jnp.dot(turned, grad_refs[j * count + count - 1][...], preferred_element_type=jnp.float32)
        total = total + jnp.dot(last_turned, grad_s[j], preferred_element_type=jnp.float32)
        out_ref[:, at] = (sum_ref[:, at] + total).astype(out_ref.dtype)


def views(refs, places):
    return [refs[which] if half is None else refs[which].at[half] for which, half in places]


def grad_operands(grads):
    arrays, places = [], []
    for array, half in grads:
        if not any(array is a for a in arrays):
            arrays.append(array)
        places.append(([i for i, a in enumerate(arrays) if a is array][0], half))
    return arrays, places


def early_sums(own, even, odd, grads, mirrors, side, size):
    rows = own.shape[1] // mirrors
    grads, places = grad_operands([g for half in grads for g in half[:-1]])
    tokens, width = grads[0].shape[-2:]
    counts = [1] + [len(parts) for parts in odd + even]
    pieces = [own] + [part for parts in odd + even for part in parts]
    return pl.pallas_call(
        functools.partial(early_kernel, size, side, counts, places),
        in_specs=[NEAR] * (len(pieces) + len(grads)),
        out_specs=NEAR,
        out_shape=jax.ShapeDtypeStruct((rows, 2 * width), jnp.float32),
        scratch_shapes=[pltpu.VMEM((len(places) // 2, tokens, rows), jnp.bfloat16)],
        cost_estimate=LENGTHY,
        compiler_params=params(24),
        name="early_sums",
    )(*pieces, *grads)


def late_sums(sums, own, even, odd, grads, mirrors, side, size, dtype):
    rows = own.shape[1] // mirrors
    grads, places = grad_operands([g for half in grads for g in half])
    tokens, width = grads[0].shape[-2:]
    counts = [1] + [len(parts) for parts in odd + even]
    pieces = [sums, own] + [part for parts in odd + even for part in parts]
    last = (len(places) // 2 - 1) * (tokens // size)
    return pl.pallas_call(
        functools.partial(late_kernel, size, side, counts, places),
        in_specs=[NEAR] * (len(pieces) + len(grads)),
        out_specs=NEAR,
        out_shape=jax.ShapeDtypeStruct((rows, 2 * width), dtype),
        scratch_shapes=[
            pltpu.VMEM((tokens, rows), jnp.bfloat16),
            pltpu.VMEM((last, rows), jnp.bfloat16),
            pltpu.VMEM((2, last, width), jnp.bfloat16),
        ],
        cost_estimate=LENGTHY,
        compiler_params=params(24),
        name="late_sums",
    )(*pieces, *grads)


def average_kernel(replicas, own_ref, *refs):
    away_refs, out_ref = refs[:-1], refs[-1]
    total = own_ref[...]
    for away_ref in away_refs:
        total = total + away_ref[...].astype(jnp.float32)
    out_ref[...] = (total * (1.0 / replicas)).reshape(out_ref.shape)


def average(own, away, replicas):
    rows, columns = own.shape
    depth = min(rows, 128)
    block = pl.BlockSpec((depth, columns), lambda i: (i, 0))
    return pl.pallas_call(
        functools.partial(average_kernel, replicas),
        grid=(rows // depth,),
        in_specs=[block] * (1 + len(away)),
        out_specs=pl.BlockSpec((depth, 2, columns // 2), lambda i: (i, 0, 0)),
        out_shape=jax.ShapeDtypeStruct((rows, 2, columns // 2), jnp.float32),
        cost_estimate=BRIEF,
        compiler_params=params(32),
        name="average_weight_grad",
    )(own, *away)


def swap(values, distance, size):
    return lax.ppermute(values, "dp", [(i, i ^ distance) for i in range(size)])


def across(values, distance, size):
    return lax.ppermute(values, "mirror", [(i, (i + distance) % size) for i in range(size)])


def gathered(grads, size):
    bits = [1 << b for b in range(size.bit_length() - 1)]
    near = {bit: swap(grads, bit, size) for bit in bits}
    found = []
    for half, order in enumerate((bits, bits[1:] + bits[:1])):
        blocks = {0: (grads, half)}
        for bit in order:
            for distance, (array, part) in list(blocks.items()):
                if distance == 0:
                    blocks[bit] = (near[bit], half)
                else:
                    moved = array if part is None else array[part]
                    blocks[distance ^ bit] = (swap(moved, bit, size), None)
        found.append([blocks[d] for d in range(size)])
    return found


def shards(layer_input, qk_weight, query_proj, key_proj, value_proj, head_grad, doc_ids):
    size = lax.axis_size("tensor")
    mirrors = lax.axis_size("mirror")
    data_count = lax.axis_size("dp")

    columns = split_columns(layer_input[0], mirrors, data_count)
    columns = [columns[0]] + [swap(columns[d], d, data_count) for d in range(1, data_count)]
    near = (3 * data_count + 3) // 4 * (layer_input.shape[2] // data_count)
    grads, weight_rows = attention_grads(
        query_proj[0], key_proj[0], value_proj[0], head_grad[0], doc_ids[0], qk_weight, near
    )
    columns, grads = lax.optimization_barrier((columns, grads))
    piece = merge_tokens(columns)
    partials = input_partials(grads, weight_rows, qk_weight, size, data_count)
    partials = partials.reshape(size, *piece.shape)

    even, odd = [(hop(piece, 0, size, mirrors),)], [(hop(piece, 1, size, mirrors),)]
    own_piece = piece
    for distance in range(size - 1, 0, -1):
        send = {}
        for part in range(PARTS):
            for parity, came in ((0, odd[-1]), (1, even[-1])):
                flow = came[part % len(came)]
                send[parity, part] = pass_on(flow, partials, parity, distance, part, PARTS)
                if distance == 1:
                    send[parity, part], own_piece = lax.optimization_barrier((send[parity, part], own_piece))
        for parity, hops in ((0, even), (1, odd)):
            hops.append(tuple(hop(send[parity, part], parity, size, mirrors) for part in range(PARTS)))

    grads = gathered(grads, data_count)
    sides = range(mirrors)
    early = [early_sums(piece, even[:-2], odd[:-2], grads, mirrors, side, size) for side in sides]
    away = []
    for side in sides[1:]:
        sums = late_sums(early[side], own_piece, even[:-1], odd[:-1], grads, mirrors, side, size, jnp.bfloat16)
        away.append(across(sums, side, mirrors))
    own = late_sums(early[0], own_piece, even[:-1], odd[:-1], grads, mirrors, 0, size, jnp.float32)
    weight_grad = average(own, away, mirrors * data_count)
    last_odd, last_even, weight_grad = lax.optimization_barrier((odd[-1], even[-1], weight_grad))
    input_grad = finish(last_even, last_odd, partials, data_count)[None]
    return (input_grad, weight_grad)


def solution(mesh):
    in_specs = (
        P(("mirror", "dp"), "tensor", None),
        P(None, None, "tensor"),
        P(("mirror", "dp"), None, "tensor"),
        P(("mirror", "dp"), None, "tensor"),
        P(("mirror", "dp"), None, "tensor"),
        P(("mirror", "dp"), None, "tensor"),
        P(("mirror", "dp"), None),
    )
    out_specs = (P(("mirror", "dp"), "tensor", None), P(("mirror", "dp"), None, "tensor"))
    return jax.shard_map(shards, mesh=mesh, in_specs=in_specs, out_specs=out_specs, check_vma=False)
```

```python
import functools
import math

import jax
import jax.numpy as jnp
import numpy as np
from jax import lax
from jax.experimental import pallas as pl
from jax.experimental.pallas import tpu as pltpu
from jax.sharding import PartitionSpec as P

HD = 128
SEQ = 128
GROUP = 4
SPAN = 1024
PARTS = 1
MIB = 1 << 20
ROWS = (((1,), (1,)), ((), ()))
COLS = (((0,), (0,)), ((), ()))
LENGTHY = pl.CostEstimate(flops=32 << 30, bytes_accessed=1 << 23, transcendentals=0)
BRIEF = pl.CostEstimate(flops=1, bytes_accessed=1, transcendentals=0)
NEAR = pl.BlockSpec(memory_space=pltpu.VMEM)
FAR = pl.BlockSpec(memory_space=pl.ANY)


def params(mib):
    return pltpu.CompilerParams(vmem_limit_bytes=mib * MIB)


def in_hbm(array):
    return pltpu.with_memory_space_constraint(array, pltpu.HBM)


def rope_tables():
    half = HD // 2
    inverse = np.exp(-(np.float32(2.0) * np.arange(half, dtype=np.float32) / np.float32(HD)) * np.float32(math.log(10000.0)))
    angles = np.arange(SEQ, dtype=np.float32)[:, None] * inverse[None, :].astype(np.float32)
    cosine, sine = np.cos(angles), np.sin(angles)
    return np.stack([np.concatenate([cosine, cosine], axis=1), np.concatenate([-sine, sine], axis=1)])


def attention_kernel(doc_ref, table_ref, q_ref, k_ref, v_ref, h_ref, w_ref, grad_ref, near_ref, doc_s, table_s, in_s, doc_sem, in_sem, w_sem):
    tokens, width = q_ref.shape
    scale = 1.0 / math.sqrt(HD)
    loads = []
    for b in range(tokens // SEQ):
        at = pl.ds(b * SEQ, SEQ)
        refs = enumerate((q_ref, k_ref, v_ref, h_ref))
        loads.append([pltpu.make_async_copy(ref.at[at], in_s.at[i, at], in_sem.at[b, i]) for i, ref in refs])
    first = [pltpu.make_async_copy(doc_ref, doc_s, doc_sem.at[0]), pltpu.make_async_copy(table_ref, table_s, doc_sem.at[1])]
    fetch = pltpu.make_async_copy(w_ref.at[pl.ds(0, near_ref.shape[0])], near_ref, w_sem)
    for copy in first + [c for load in loads for c in load] + [fetch]:
        copy.start()
    for copy in first:
        copy.wait()

    cosine, sine = table_s[0], table_s[1]
    back_cosine, back_sine = cosine * scale, sine * scale
    row = lax.broadcasted_iota(jnp.int32, (SEQ, SEQ), 0)
    col = lax.broadcasted_iota(jnp.int32, (SEQ, SEQ), 1)

    def rope(values):
        values = values.astype(jnp.float32)
        return (values * cosine + pltpu.roll(values, HD // 2, 1) * sine).astype(jnp.bfloat16)

    def unrope(values):
        return (values * back_cosine - pltpu.roll(values, HD // 2, 1) * back_sine).astype(jnp.bfloat16)

    for b in range(tokens // SEQ):
        rows = slice(b * SEQ, (b + 1) * SEQ)
        queries = lax.broadcast_in_dim(doc_s[b], (SEQ, SEQ), (0, 1))
        allowed = (row <= col) & (queries == queries.T)
        for copy in loads[b]:
            copy.wait()
        for first in range(0, width // HD, GROUP):
            ats = [slice(h * HD, (h + 1) * HD) for h in range(first, min(first + GROUP, width // HD))]
            q_rot = [rope(in_s[0, rows, at]) for at in ats]
            k_rot = [rope(in_s[1, rows, at]) for at in ats]
            scores = [
                lax.dot_general(k, q, ROWS, preferred_element_type=jnp.float32) for q, k in zip(q_rot, k_rot)
            ]
            dprob = [
                lax.dot_general(in_s[2, rows, at], in_s[3, rows, at], ROWS, preferred_element_type=jnp.float32)
                for at in ats
            ]
            scores = [jnp.where(allowed, s, -1e30) for s in scores]
            exps = [
                jnp.exp2((s - jnp.max(s, axis=0, keepdims=True)) * (scale * math.log2(math.e))) for s in scores
            ]
            probs = [e * (1.0 / jnp.sum(e, axis=0, keepdims=True)) for e in exps]
            dscore = [
                (p * (d - jnp.sum(p * d, axis=0, keepdims=True))).astype(jnp.bfloat16)
                for p, d in zip(probs, dprob)
            ]
            for at, ds, q, k in zip(ats, dscore, q_rot, k_rot):
                grad_ref[0, rows, at] = unrope(lax.dot_general(ds, k, COLS, preferred_element_type=jnp.float32))
                grad_ref[1, rows, at] = unrope(jnp.dot(ds, q, preferred_element_type=jnp.float32))
    fetch.wait()


def attention_grads(query, key, value, grad, docs, weight, near):
    tokens, width = query.shape
    micro = tokens // SEQ
    return pl.pallas_call(
        attention_kernel,
        in_specs=[FAR] * 7,
        out_specs=[NEAR, NEAR],
        out_shape=[
            pltpu.VMEM((2, tokens, width), jnp.bfloat16),
            pltpu.VMEM((near, *weight.shape[1:]), jnp.bfloat16),
        ],
        scratch_shapes=[
            pltpu.VMEM((micro, 1, SEQ), jnp.int32),
            pltpu.VMEM((2, SEQ, HD), jnp.float32),
            pltpu.VMEM((4, tokens, width), jnp.bfloat16),
            pltpu.SemaphoreType.DMA((2,)),
            pltpu.SemaphoreType.DMA((micro, 4)),
            pltpu.SemaphoreType.DMA(()),
        ],
        cost_estimate=BRIEF,
        compiler_params=params(20),
        name="attention_grads",
    )(
        *(in_hbm(a) for a in (docs.reshape(micro, 1, SEQ), jnp.asarray(rope_tables()), query, key, value, grad, weight))
    )


def partials_kernel(pieces, grad_ref, near_ref, w_ref, out_ref, w_s, w_sem):
    owners, blocks, own_tokens, columns = out_ref.shape
    width = w_ref.shape[2]
    near = near_ref.shape[0] // columns
    depth = columns // pieces
    fetches = []
    for c in range((blocks - near) * pieces):
        source = w_ref.at[pl.ds(near * columns + c * depth, depth)]
        fetches.append(pltpu.make_async_copy(source, w_s.at[pl.ds(c * depth, depth)], w_sem.at[c]))
    for copy in fetches:
        copy.start()
    for start, ref in ((0, near_ref), (near, w_s)):
        if start:
            for copy in fetches:
                copy.wait()
        count = ref.shape[0] // columns
        step = min(count, max(1, SPAN // columns))
        for block in range(0, count, step):
            span = min(step, count - block) * columns
            weights = ref[block * columns : block * columns + span].reshape(span, 2 * width)
            out = lax.dot_general(grad_ref[0], weights[:, :width], ROWS, preferred_element_type=jnp.float32)
            out = out + lax.dot_general(grad_ref[1], weights[:, width:], ROWS, preferred_element_type=jnp.float32)
            out = out.astype(jnp.bfloat16)
            for at in range(span // columns):
                rows = out[:, at * columns : (at + 1) * columns]
                out_ref[:, start + block + at] = rows.reshape(owners, own_tokens, columns)


def input_partials(grads, near, weight, owners, blocks):
    _, tokens, width = grads.shape
    model = weight.shape[0]
    pieces = 2
    left = model - near.shape[0]
    return pl.pallas_call(
        functools.partial(partials_kernel, pieces),
        in_specs=[NEAR, NEAR, FAR],
        out_specs=NEAR,
        out_shape=pltpu.VMEM((owners, blocks, tokens // owners, model // blocks), jnp.bfloat16),
        scratch_shapes=[
            pltpu.VMEM((left, *weight.shape[1:]), jnp.bfloat16),
            pltpu.SemaphoreType.DMA((left * blocks * pieces // model,)),
        ],
        cost_estimate=BRIEF,
        compiler_params=params(36),
        name="input_partials",
    )(grads, near, in_hbm(weight))


def split_kernel(mirrors, x_ref, *refs):
    out_refs, sem = refs[:-1], refs[-1]
    data_count = len(out_refs)
    width = x_ref.shape[1] // (mirrors * data_count)
    copies = []
    for distance, out_ref in enumerate(out_refs):
        owner = lax.axis_index("dp") ^ distance
        for k in range(mirrors):
            block = lax.rem(lax.axis_index("mirror") + k, mirrors) * data_count + owner
            source = x_ref.at[:, pl.ds(pl.multiple_of(block * width, width), width)]
            target = out_ref.at[:, pl.ds(k * width, width)]
            copies.append(pltpu.make_async_copy(source, target, sem.at[distance, k]))
    for copy in copies:
        copy.start()
    for copy in copies:
        copy.wait()


def split_columns(rows, mirrors, data_count):
    tokens, model = rows.shape
    out = jax.ShapeDtypeStruct((tokens, model // data_count), rows.dtype)
    return pl.pallas_call(
        functools.partial(split_kernel, mirrors),
        in_specs=[FAR],
        out_specs=[FAR] * data_count,
        out_shape=[out] * data_count,
        scratch_shapes=[pltpu.SemaphoreType.DMA((data_count, mirrors))],
        cost_estimate=BRIEF,
        compiler_params=params(16),
        name="split_columns",
    )(in_hbm(rows))


def merge_kernel(*refs):
    in_refs, out_ref = refs[:-1], refs[-1]
    tokens = in_refs[0].shape[0]
    for i, in_ref in enumerate(in_refs):
        out_ref[i * tokens : (i + 1) * tokens, :] = in_ref[...]


def merge_tokens(columns):
    tokens, width = columns[0].shape
    return pl.pallas_call(
        merge_kernel,
        in_specs=[NEAR] * len(columns),
        out_specs=NEAR,
        out_shape=jax.ShapeDtypeStruct((len(columns) * tokens, width), columns[0].dtype),
        cost_estimate=BRIEF,
        compiler_params=params(16),
        name="merge_tokens",
    )(*columns)


def hop(values, parity, size, mirrors):
    pairs = []
    for i in range(size):
        j = i + 1 if i % 2 == parity else i - 1
        for r in range(mirrors):
            to = (j, r) if 0 <= j < size else (i, (r + 1) % mirrors)
            pairs.append((i * mirrors + r, to[0] * mirrors + to[1]))
    return lax.ppermute(values, ("tensor", "mirror"), pairs)


def has_partner(me, parity, size):
    ahead = lax.rem(me, 2) == parity
    partner = jnp.where(ahead, me + 1, me - 1)
    return (partner >= 0) & (partner < size), ahead


def pass_kernel(parity, distance, part, flow_ref, partial_ref, out_ref):
    size = partial_ref.shape[0]
    me = lax.axis_index("tensor")
    ahead = lax.rem(me, 2) == parity
    owner = jnp.where(ahead, me + distance, me - distance)
    active = (owner >= 0) & (owner < size)
    flows, _ = has_partner(me, 1 - parity, size)
    owner = jnp.clip(owner, 0, size - 1)
    height = out_ref.shape[0]
    rows = slice(part * height, (part + 1) * height)
    flow_rows = rows if flow_ref.shape[0] > height else slice(0, height)

    @pl.when(flows & active)
    def _():
        out_ref[...] = flow_ref[flow_rows] + partial_ref[owner, rows]

    @pl.when(jnp.logical_not(flows))
    def _():
        out_ref[...] = partial_ref[owner, rows]

    @pl.when(flows & jnp.logical_not(active))
    def _():
        out_ref[...] = flow_ref[flow_rows]


def pass_on(flow, partials, parity, distance, part, parts):
    _, rows, columns = partials.shape
    return pl.pallas_call(
        functools.partial(pass_kernel, parity, distance, part),
        in_specs=[NEAR, NEAR],
        out_specs=NEAR,
        out_shape=jax.ShapeDtypeStruct((rows // parts, columns), partials.dtype),
        cost_estimate=BRIEF,
        compiler_params=params(16),
        name="pass_on",
    )(flow, partials)


def finish_kernel(blocks, parts, *refs):
    odd_refs, even_refs, (partial_ref, out_ref, out_s, sem) = refs[:parts], refs[parts : 2 * parts], refs[2 * parts :]
    size = partial_ref.shape[0]
    me = lax.axis_index("tensor")
    tokens, columns = out_ref.shape[0], out_ref.shape[1] // blocks
    has_even, has_odd = (has_partner(me, parity, size)[0] for parity in range(2))

    def store_block(block):
        at = pl.ds(block * columns, columns)
        return pltpu.make_async_copy(out_s.at[:, at], out_ref.at[:, at], sem.at[block])

    def store(*flows):
        for block in range(blocks):
            per = blocks // parts
            rows = slice(block % per * tokens, (block % per + 1) * tokens)
            total = partial_ref[me, block * tokens : (block + 1) * tokens].astype(jnp.float32)
            for refs in flows:
                total = total + refs[block // per][rows].astype(jnp.float32)
            out_s[:, block * columns : (block + 1) * columns] = total.astype(out_s.dtype)
            store_block(block).start()

    @pl.when(has_even & has_odd)
    def _():
        store(even_refs, odd_refs)

    @pl.when(jnp.logical_not(has_odd))
    def _():
        store(even_refs)

    @pl.when(jnp.logical_not(has_even))
    def _():
        store(odd_refs)

    for block in range(blocks):
        store_block(block).wait()


def finish(even, odd, partials, blocks):
    _, rows, columns = partials.shape
    return pl.pallas_call(
        functools.partial(finish_kernel, blocks, len(even)),
        in_specs=[NEAR] * (2 * len(even) + 1),
        out_specs=FAR,
        out_shape=jax.ShapeDtypeStruct((rows // blocks, columns * blocks), partials.dtype),
        scratch_shapes=[
            pltpu.VMEM((rows // blocks, columns * blocks), partials.dtype),
            pltpu.SemaphoreType.DMA((blocks,)),
        ],
        cost_estimate=BRIEF,
        compiler_params=params(16),
        name="finish_input_grad",
    )(*odd, *even, partials)


def grouped(refs, counts):
    groups, at = [], 0
    for count in counts:
        groups.append(refs[at : at + count])
        at += count
    return groups


def replica_rows(parts, k, own_tokens):
    height = parts[0].shape[0]
    start = k * own_tokens % height
    return parts[k * own_tokens // height], slice(start, start + own_tokens)


def piece_cases(me, size, even_refs, odd_refs):
    odd_place = lax.rem(me, 2) == 1
    even_place = jnp.logical_not(odd_place)
    cases = []
    for slot in range(1, size):
        behind = me >= slot
        beyond = jnp.logical_not(behind)
        back = size - slot
        cases.append(
            (
                (behind & odd_place, even_refs, slot),
                (behind & even_place, odd_refs, slot),
                (beyond & odd_place, odd_refs, back),
                (beyond & even_place, even_refs, back),
            )
        )
    return [[(c, refs[hop - 1] if hop <= len(refs) else None, hop == size - 1) for c, refs, hop in case] for case in cases]


def early_kernel(size, side, counts, places, *refs):
    out_ref, x_s = refs[-2:]
    pieces = grouped(refs[: sum(counts)], counts)
    own_ref, odd_refs, even_refs = pieces[0], pieces[1 : size - 1], pieces[size - 1 :]
    grad_refs = views(refs[sum(counts) : -2], places)
    count = len(grad_refs) // 2
    me = lax.axis_index("tensor")
    tokens, rows = x_s.shape[1:]
    own_tokens = tokens // size
    width = out_ref.shape[1] // 2

    def place(ref, slot):
        start = pl.multiple_of(lax.rem(me - slot + size, size) * own_tokens, own_tokens)
        for k in range(count):
            if ref is None:
                values = jnp.zeros((own_tokens, rows), x_s.dtype)
            else:
                part, at = replica_rows(ref, k, own_tokens)
                values = part[at, side * rows : (side + 1) * rows]
            x_s[k, pl.ds(start, own_tokens), :] = values

    place(own_ref, 0)
    for slot, case in enumerate(piece_cases(me, size, even_refs, odd_refs), 1):
        for condition, ref, _ in case:

            @pl.when(condition)
            def _(ref=ref, slot=slot):
                place(ref, slot)

    turned = [x_s[k].T for k in range(count)]
    for j in range(2):
        total = None
        for k in range(count):
            term = jnp.dot(turned[k], grad_refs[j * count + k][...], preferred_element_type=jnp.float32)
            total = term if total is None else total + term
        out_ref[:, j * width : (j + 1) * width] = total


def late_kernel(size, side, counts, places, *refs):
    sum_ref, refs = refs[0], refs[1:]
    out_ref, x_s, last_s, grad_s = refs[-4:]
    pieces = grouped(refs[: sum(counts)], counts)
    own_ref, odd_refs, even_refs = pieces[0], pieces[1:size], pieces[size:]
    grad_refs = views(refs[sum(counts) : -4], places)
    count = len(grad_refs) // 2
    me = lax.axis_index("tensor")
    tokens, rows = x_s.shape
    own_tokens = tokens // size
    width = out_ref.shape[1] // 2
    columns = slice(side * rows, (side + 1) * rows)

    def place(ref, slot):
        start = pl.multiple_of(lax.rem(me - slot + size, size) * own_tokens, own_tokens)
        part, at = replica_rows(ref, count - 1, own_tokens)
        x_s[pl.ds(start, own_tokens), :] = part[at, columns]

    place(own_ref, 0)
    last_s[...] = jnp.zeros_like(last_s)
    for slot, case in enumerate(piece_cases(me, size, even_refs, odd_refs), 1):
        for condition, ref, last in case:

            @pl.when(condition)
            def _(ref=ref, slot=slot, last=last):
                place(ref, slot)
                if last:
                    for k in range(count - 1):
                        part, at = replica_rows(ref, k, own_tokens)
                        last_s[k * own_tokens : (k + 1) * own_tokens, :] = part[at, columns]

    owner = jnp.where(me == 0, size - 1, 0)
    start = pl.multiple_of(owner * own_tokens, own_tokens)
    for j in range(2):
        for k in range(count - 1):
            grad_s[j, k * own_tokens : (k + 1) * own_tokens, :] = grad_refs[j * count + k][pl.ds(start, own_tokens), :]
    turned, last_turned = x_s[...].T, last_s[...].T
    for j in range(2):
        at = slice(j * width, (j + 1) * width)
        total = jnp.dot(turned, grad_refs[j * count + count - 1][...], preferred_element_type=jnp.float32)
        total = total + jnp.dot(last_turned, grad_s[j], preferred_element_type=jnp.float32)
        out_ref[:, at] = (sum_ref[:, at] + total).astype(out_ref.dtype)


def views(refs, places):
    return [refs[which] if half is None else refs[which].at[half] for which, half in places]


def grad_operands(grads):
    arrays, places = [], []
    for array, half in grads:
        if not any(array is a for a in arrays):
            arrays.append(array)
        places.append(([i for i, a in enumerate(arrays) if a is array][0], half))
    return arrays, places


def early_sums(own, even, odd, grads, mirrors, side, size):
    rows = own.shape[1] // mirrors
    grads, places = grad_operands([g for half in grads for g in half[:-1]])
    tokens, width = grads[0].shape[-2:]
    counts = [1] + [len(parts) for parts in odd + even]
    pieces = [own] + [part for parts in odd + even for part in parts]
    return pl.pallas_call(
        functools.partial(early_kernel, size, side, counts, places),
        in_specs=[NEAR] * (len(pieces) + len(grads)),
        out_specs=NEAR,
        out_shape=jax.ShapeDtypeStruct((rows, 2 * width), jnp.float32),
        scratch_shapes=[pltpu.VMEM((len(places) // 2, tokens, rows), jnp.bfloat16)],
        cost_estimate=LENGTHY,
        compiler_params=params(24),
        name="early_sums",
    )(*pieces, *grads)


def late_sums(sums, own, even, odd, grads, mirrors, side, size, dtype):
    rows = own.shape[1] // mirrors
    grads, places = grad_operands([g for half in grads for g in half])
    tokens, width = grads[0].shape[-2:]
    counts = [1] + [len(parts) for parts in odd + even]
    pieces = [sums, own] + [part for parts in odd + even for part in parts]
    last = (len(places) // 2 - 1) * (tokens // size)
    return pl.pallas_call(
        functools.partial(late_kernel, size, side, counts, places),
        in_specs=[NEAR] * (len(pieces) + len(grads)),
        out_specs=NEAR,
        out_shape=jax.ShapeDtypeStruct((rows, 2 * width), dtype),
        scratch_shapes=[
            pltpu.VMEM((tokens, rows), jnp.bfloat16),
            pltpu.VMEM((last, rows), jnp.bfloat16),
            pltpu.VMEM((2, last, width), jnp.bfloat16),
        ],
        cost_estimate=LENGTHY,
        compiler_params=params(24),
        name="late_sums",
    )(*pieces, *grads)


def average_kernel(replicas, own_ref, *refs):
    away_refs, out_ref = refs[:-1], refs[-1]
    total = own_ref[...]
    for away_ref in away_refs:
        total = total + away_ref[...].astype(jnp.float32)
    out_ref[...] = (total * (1.0 / replicas)).reshape(out_ref.shape)


def average(own, away, replicas):
    rows, columns = own.shape
    depth = min(rows, 128)
    block = pl.BlockSpec((depth, columns), lambda i: (i, 0))
    return pl.pallas_call(
        functools.partial(average_kernel, replicas),
        grid=(rows // depth,),
        in_specs=[block] * (1 + len(away)),
        out_specs=pl.BlockSpec((depth, 2, columns // 2), lambda i: (i, 0, 0)),
        out_shape=jax.ShapeDtypeStruct((rows, 2, columns // 2), jnp.float32),
        cost_estimate=BRIEF,
        compiler_params=params(32),
        name="average_weight_grad",
    )(own, *away)


def swap(values, distance, size):
    return lax.ppermute(values, "dp", [(i, i ^ distance) for i in range(size)])


def across(values, distance, size):
    return lax.ppermute(values, "mirror", [(i, (i + distance) % size) for i in range(size)])


def gathered(grads, size):
    bits = [1 << b for b in range(size.bit_length() - 1)]
    near = {bit: swap(grads, bit, size) for bit in bits}
    found = []
    for half, order in enumerate((bits, bits[1:] + bits[:1])):
        blocks = {0: (grads, half)}
        for bit in order:
            for distance, (array, part) in list(blocks.items()):
                if distance == 0:
                    blocks[bit] = (near[bit], half)
                else:
                    moved = array if part is None else array[part]
                    blocks[distance ^ bit] = (swap(moved, bit, size), None)
        found.append([blocks[d] for d in range(size)])
    return found


def shards(layer_input, qk_weight, query_proj, key_proj, value_proj, head_grad, doc_ids):
    size = lax.axis_size("tensor")
    mirrors = lax.axis_size("mirror")
    data_count = lax.axis_size("dp")

    columns = split_columns(layer_input[0], mirrors, data_count)
    columns = [columns[0]] + [swap(columns[d], d, data_count) for d in range(1, data_count)]
    near = 3 * data_count // 4 * (layer_input.shape[2] // data_count)
    grads, weight_rows = attention_grads(
        query_proj[0], key_proj[0], value_proj[0], head_grad[0], doc_ids[0], qk_weight, near
    )
    columns, grads = lax.optimization_barrier((columns, grads))
    piece = merge_tokens(columns)
    partials = input_partials(grads, weight_rows, qk_weight, size, data_count)
    partials = partials.reshape(size, *piece.shape)

    even, odd = [(hop(piece, 0, size, mirrors),)], [(hop(piece, 1, size, mirrors),)]
    own_piece = piece
    for distance in range(size - 1, 0, -1):
        send = {}
        for part in range(PARTS):
            for parity, came in ((0, odd[-1]), (1, even[-1])):
                flow = came[part % len(came)]
                send[parity, part] = pass_on(flow, partials, parity, distance, part, PARTS)
                if distance == 1:
                    send[parity, part], own_piece = lax.optimization_barrier((send[parity, part], own_piece))
        for parity, hops in ((0, even), (1, odd)):
            hops.append(tuple(hop(send[parity, part], parity, size, mirrors) for part in range(PARTS)))

    grads = gathered(grads, data_count)
    sides = range(mirrors)
    early = [early_sums(piece, even[:-2], odd[:-2], grads, mirrors, side, size) for side in sides]
    away = []
    for side in sides[1:]:
        sums = late_sums(early[side], own_piece, even[:-1], odd[:-1], grads, mirrors, side, size, jnp.bfloat16)
        away.append(across(sums, side, mirrors))
    own = late_sums(early[0], own_piece, even[:-1], odd[:-1], grads, mirrors, 0, size, jnp.float32)
    weight_grad = average(own, away, mirrors * data_count)
    last_odd, last_even, weight_grad = lax.optimization_barrier((odd[-1], even[-1], weight_grad))
    input_grad = finish(last_even, last_odd, partials, data_count)[None]
    return (input_grad, weight_grad)


def solution(mesh):
    in_specs = (
        P(("mirror", "dp"), "tensor", None),
        P(None, None, "tensor"),
        P(("mirror", "dp"), None, "tensor"),
        P(("mirror", "dp"), None, "tensor"),
        P(("mirror", "dp"), None, "tensor"),
        P(("mirror", "dp"), None, "tensor"),
        P(("mirror", "dp"), None),
    )
    out_specs = (P(("mirror", "dp"), "tensor", None), P(("mirror", "dp"), None, "tensor"))
    return jax.shard_map(shards, mesh=mesh, in_specs=in_specs, out_specs=out_specs, check_vma=False)
```

```python
import functools
import math

import jax
import jax.numpy as jnp
import numpy as np
from jax import lax
from jax.experimental import pallas as pl
from jax.experimental.pallas import tpu as pltpu
from jax.sharding import PartitionSpec as P

HD = 128
SEQ = 128
GROUP = 4
SPAN = 3072
PARTS = 1
MIB = 1 << 20
ROWS = (((1,), (1,)), ((), ()))
COLS = (((0,), (0,)), ((), ()))
LENGTHY = pl.CostEstimate(flops=32 << 30, bytes_accessed=1 << 23, transcendentals=0)
BRIEF = pl.CostEstimate(flops=1, bytes_accessed=1, transcendentals=0)
NEAR = pl.BlockSpec(memory_space=pltpu.VMEM)
FAR = pl.BlockSpec(memory_space=pl.ANY)


def params(mib):
    return pltpu.CompilerParams(vmem_limit_bytes=mib * MIB)


def in_hbm(array):
    return pltpu.with_memory_space_constraint(array, pltpu.HBM)


def rope_tables():
    half = HD // 2
    inverse = np.exp(-(np.float32(2.0) * np.arange(half, dtype=np.float32) / np.float32(HD)) * np.float32(math.log(10000.0)))
    angles = np.arange(SEQ, dtype=np.float32)[:, None] * inverse[None, :].astype(np.float32)
    cosine, sine = np.cos(angles), np.sin(angles)
    return np.stack([np.concatenate([cosine, cosine], axis=1), np.concatenate([-sine, sine], axis=1)])


def attention_kernel(doc_ref, table_ref, q_ref, k_ref, v_ref, h_ref, w_ref, grad_ref, near_ref, doc_s, table_s, in_s, doc_sem, in_sem, w_sem):
    tokens, width = q_ref.shape
    scale = 1.0 / math.sqrt(HD)
    loads = []
    for b in range(tokens // SEQ):
        at = pl.ds(b * SEQ, SEQ)
        refs = enumerate((q_ref, k_ref, v_ref, h_ref))
        loads.append([pltpu.make_async_copy(ref.at[at], in_s.at[i, at], in_sem.at[b, i]) for i, ref in refs])
    first = [pltpu.make_async_copy(doc_ref, doc_s, doc_sem.at[0]), pltpu.make_async_copy(table_ref, table_s, doc_sem.at[1])]
    fetch = pltpu.make_async_copy(w_ref.at[pl.ds(0, near_ref.shape[0])], near_ref, w_sem)
    for copy in first + [c for load in loads for c in load] + [fetch]:
        copy.start()
    for copy in first:
        copy.wait()

    cosine, sine = table_s[0], table_s[1]
    back_cosine, back_sine = cosine * scale, sine * scale
    row = lax.broadcasted_iota(jnp.int32, (SEQ, SEQ), 0)
    col = lax.broadcasted_iota(jnp.int32, (SEQ, SEQ), 1)

    def rope(values):
        values = values.astype(jnp.float32)
        return (values * cosine + pltpu.roll(values, HD // 2, 1) * sine).astype(jnp.bfloat16)

    def unrope(values):
        return (values * back_cosine - pltpu.roll(values, HD // 2, 1) * back_sine).astype(jnp.bfloat16)

    for b in range(tokens // SEQ):
        rows = slice(b * SEQ, (b + 1) * SEQ)
        queries = lax.broadcast_in_dim(doc_s[b], (SEQ, SEQ), (0, 1))
        allowed = (row <= col) & (queries == queries.T)
        for copy in loads[b]:
            copy.wait()
        for first in range(0, width // HD, GROUP):
            ats = [slice(h * HD, (h + 1) * HD) for h in range(first, min(first + GROUP, width // HD))]
            q_rot = [rope(in_s[0, rows, at]) for at in ats]
            k_rot = [rope(in_s[1, rows, at]) for at in ats]
            scores = [
                lax.dot_general(k, q, ROWS, preferred_element_type=jnp.float32) for q, k in zip(q_rot, k_rot)
            ]
            dprob = [
                lax.dot_general(in_s[2, rows, at], in_s[3, rows, at], ROWS, preferred_element_type=jnp.float32)
                for at in ats
            ]
            scores = [jnp.where(allowed, s, -1e30) for s in scores]
            exps = [
                jnp.exp2((s - jnp.max(s, axis=0, keepdims=True)) * (scale * math.log2(math.e))) for s in scores
            ]
            probs = [e * (1.0 / jnp.sum(e, axis=0, keepdims=True)) for e in exps]
            dscore = [
                (p * (d - jnp.sum(p * d, axis=0, keepdims=True))).astype(jnp.bfloat16)
                for p, d in zip(probs, dprob)
            ]
            for at, ds, q, k in zip(ats, dscore, q_rot, k_rot):
                grad_ref[0, rows, at] = unrope(lax.dot_general(ds, k, COLS, preferred_element_type=jnp.float32))
                grad_ref[1, rows, at] = unrope(jnp.dot(ds, q, preferred_element_type=jnp.float32))
    fetch.wait()


def attention_grads(query, key, value, grad, docs, weight, near):
    tokens, width = query.shape
    micro = tokens // SEQ
    return pl.pallas_call(
        attention_kernel,
        in_specs=[FAR] * 7,
        out_specs=[NEAR, NEAR],
        out_shape=[
            pltpu.VMEM((2, tokens, width), jnp.bfloat16),
            pltpu.VMEM((near, *weight.shape[1:]), jnp.bfloat16),
        ],
        scratch_shapes=[
            pltpu.VMEM((micro, 1, SEQ), jnp.int32),
            pltpu.VMEM((2, SEQ, HD), jnp.float32),
            pltpu.VMEM((4, tokens, width), jnp.bfloat16),
            pltpu.SemaphoreType.DMA((2,)),
            pltpu.SemaphoreType.DMA((micro, 4)),
            pltpu.SemaphoreType.DMA(()),
        ],
        cost_estimate=BRIEF,
        compiler_params=params(20),
        name="attention_grads",
    )(
        *(in_hbm(a) for a in (docs.reshape(micro, 1, SEQ), jnp.asarray(rope_tables()), query, key, value, grad, weight))
    )


def partials_kernel(pieces, grad_ref, near_ref, w_ref, out_ref, w_s, w_sem):
    owners, blocks, own_tokens, columns = out_ref.shape
    width = w_ref.shape[2]
    near = near_ref.shape[0] // columns
    depth = columns // pieces
    fetches = []
    for c in range((blocks - near) * pieces):
        source = w_ref.at[pl.ds(near * columns + c * depth, depth)]
        fetches.append(pltpu.make_async_copy(source, w_s.at[pl.ds(c * depth, depth)], w_sem.at[c]))
    for copy in fetches:
        copy.start()
    for start, ref in ((0, near_ref), (near, w_s)):
        if start:
            for copy in fetches:
                copy.wait()
        count = ref.shape[0] // columns
        step = min(count, max(1, SPAN // columns))
        for block in range(0, count, step):
            span = min(step, count - block) * columns
            weights = ref[block * columns : block * columns + span].reshape(span, 2 * width)
            out = lax.dot_general(grad_ref[0], weights[:, :width], ROWS, preferred_element_type=jnp.float32)
            out = out + lax.dot_general(grad_ref[1], weights[:, width:], ROWS, preferred_element_type=jnp.float32)
            out = out.astype(jnp.bfloat16)
            for at in range(span // columns):
                rows = out[:, at * columns : (at + 1) * columns]
                out_ref[:, start + block + at] = rows.reshape(owners, own_tokens, columns)


def input_partials(grads, near, weight, owners, blocks):
    _, tokens, width = grads.shape
    model = weight.shape[0]
    pieces = 2
    left = model - near.shape[0]
    return pl.pallas_call(
        functools.partial(partials_kernel, pieces),
        in_specs=[NEAR, NEAR, FAR],
        out_specs=NEAR,
        out_shape=pltpu.VMEM((owners, blocks, tokens // owners, model // blocks), jnp.bfloat16),
        scratch_shapes=[
            pltpu.VMEM((left, *weight.shape[1:]), jnp.bfloat16),
            pltpu.SemaphoreType.DMA((left * blocks * pieces // model,)),
        ],
        cost_estimate=BRIEF,
        compiler_params=params(36),
        name="input_partials",
    )(grads, near, in_hbm(weight))


def split_kernel(mirrors, x_ref, *refs):
    out_refs, sem = refs[:-1], refs[-1]
    data_count = len(out_refs)
    width = x_ref.shape[1] // (mirrors * data_count)
    copies = []
    for distance, out_ref in enumerate(out_refs):
        owner = lax.axis_index("dp") ^ distance
        for k in range(mirrors):
            block = lax.rem(lax.axis_index("mirror") + k, mirrors) * data_count + owner
            source = x_ref.at[:, pl.ds(pl.multiple_of(block * width, width), width)]
            target = out_ref.at[:, pl.ds(k * width, width)]
            copies.append(pltpu.make_async_copy(source, target, sem.at[distance, k]))
    for copy in copies:
        copy.start()
    for copy in copies:
        copy.wait()


def split_columns(rows, mirrors, data_count):
    tokens, model = rows.shape
    out = jax.ShapeDtypeStruct((tokens, model // data_count), rows.dtype)
    return pl.pallas_call(
        functools.partial(split_kernel, mirrors),
        in_specs=[FAR],
        out_specs=[FAR] * data_count,
        out_shape=[out] * data_count,
        scratch_shapes=[pltpu.SemaphoreType.DMA((data_count, mirrors))],
        cost_estimate=BRIEF,
        compiler_params=params(16),
        name="split_columns",
    )(in_hbm(rows))


def merge_kernel(*refs):
    in_refs, out_ref = refs[:-1], refs[-1]
    tokens = in_refs[0].shape[0]
    for i, in_ref in enumerate(in_refs):
        out_ref[i * tokens : (i + 1) * tokens, :] = in_ref[...]


def merge_tokens(columns):
    tokens, width = columns[0].shape
    return pl.pallas_call(
        merge_kernel,
        in_specs=[NEAR] * len(columns),
        out_specs=NEAR,
        out_shape=jax.ShapeDtypeStruct((len(columns) * tokens, width), columns[0].dtype),
        cost_estimate=BRIEF,
        compiler_params=params(16),
        name="merge_tokens",
    )(*columns)


def hop(values, parity, size, mirrors):
    pairs = []
    for i in range(size):
        j = i + 1 if i % 2 == parity else i - 1
        for r in range(mirrors):
            to = (j, r) if 0 <= j < size else (i, (r + 1) % mirrors)
            pairs.append((i * mirrors + r, to[0] * mirrors + to[1]))
    return lax.ppermute(values, ("tensor", "mirror"), pairs)


def has_partner(me, parity, size):
    ahead = lax.rem(me, 2) == parity
    partner = jnp.where(ahead, me + 1, me - 1)
    return (partner >= 0) & (partner < size), ahead


def pass_kernel(parity, distance, part, flow_ref, partial_ref, out_ref):
    size = partial_ref.shape[0]
    me = lax.axis_index("tensor")
    ahead = lax.rem(me, 2) == parity
    owner = jnp.where(ahead, me + distance, me - distance)
    active = (owner >= 0) & (owner < size)
    flows, _ = has_partner(me, 1 - parity, size)
    owner = jnp.clip(owner, 0, size - 1)
    height = out_ref.shape[0]
    rows = slice(part * height, (part + 1) * height)
    flow_rows = rows if flow_ref.shape[0] > height else slice(0, height)

    @pl.when(flows & active)
    def _():
        out_ref[...] = flow_ref[flow_rows] + partial_ref[owner, rows]

    @pl.when(jnp.logical_not(flows))
    def _():
        out_ref[...] = partial_ref[owner, rows]

    @pl.when(flows & jnp.logical_not(active))
    def _():
        out_ref[...] = flow_ref[flow_rows]


def pass_on(flow, partials, parity, distance, part, parts):
    _, rows, columns = partials.shape
    return pl.pallas_call(
        functools.partial(pass_kernel, parity, distance, part),
        in_specs=[NEAR, NEAR],
        out_specs=NEAR,
        out_shape=jax.ShapeDtypeStruct((rows // parts, columns), partials.dtype),
        cost_estimate=BRIEF,
        compiler_params=params(16),
        name="pass_on",
    )(flow, partials)


def finish_kernel(blocks, parts, *refs):
    odd_refs, even_refs, (partial_ref, out_ref, out_s, sem) = refs[:parts], refs[parts : 2 * parts], refs[2 * parts :]
    size = partial_ref.shape[0]
    me = lax.axis_index("tensor")
    tokens, columns = out_ref.shape[0], out_ref.shape[1] // blocks
    has_even, has_odd = (has_partner(me, parity, size)[0] for parity in range(2))

    def store_block(block):
        at = pl.ds(block * columns, columns)
        return pltpu.make_async_copy(out_s.at[:, at], out_ref.at[:, at], sem.at[block])

    def store(*flows):
        for block in range(blocks):
            per = blocks // parts
            rows = slice(block % per * tokens, (block % per + 1) * tokens)
            total = partial_ref[me, block * tokens : (block + 1) * tokens].astype(jnp.float32)
            for refs in flows:
                total = total + refs[block // per][rows].astype(jnp.float32)
            out_s[:, block * columns : (block + 1) * columns] = total.astype(out_s.dtype)
            store_block(block).start()

    @pl.when(has_even & has_odd)
    def _():
        store(even_refs, odd_refs)

    @pl.when(jnp.logical_not(has_odd))
    def _():
        store(even_refs)

    @pl.when(jnp.logical_not(has_even))
    def _():
        store(odd_refs)

    for block in range(blocks):
        store_block(block).wait()


def finish(even, odd, partials, blocks):
    _, rows, columns = partials.shape
    return pl.pallas_call(
        functools.partial(finish_kernel, blocks, len(even)),
        in_specs=[NEAR] * (2 * len(even) + 1),
        out_specs=FAR,
        out_shape=jax.ShapeDtypeStruct((rows // blocks, columns * blocks), partials.dtype),
        scratch_shapes=[
            pltpu.VMEM((rows // blocks, columns * blocks), partials.dtype),
            pltpu.SemaphoreType.DMA((blocks,)),
        ],
        cost_estimate=BRIEF,
        compiler_params=params(16),
        name="finish_input_grad",
    )(*odd, *even, partials)


def grouped(refs, counts):
    groups, at = [], 0
    for count in counts:
        groups.append(refs[at : at + count])
        at += count
    return groups


def replica_rows(parts, k, own_tokens):
    height = parts[0].shape[0]
    start = k * own_tokens % height
    return parts[k * own_tokens // height], slice(start, start + own_tokens)


def piece_cases(me, size, even_refs, odd_refs):
    odd_place = lax.rem(me, 2) == 1
    even_place = jnp.logical_not(odd_place)
    cases = []
    for slot in range(1, size):
        behind = me >= slot
        beyond = jnp.logical_not(behind)
        back = size - slot
        cases.append(
            (
                (behind & odd_place, even_refs, slot),
                (behind & even_place, odd_refs, slot),
                (beyond & odd_place, odd_refs, back),
                (beyond & even_place, even_refs, back),
            )
        )
    return [[(c, refs[hop - 1] if hop <= len(refs) else None, hop == size - 1) for c, refs, hop in case] for case in cases]


def early_kernel(size, side, counts, places, *refs):
    out_ref, x_s = refs[-2:]
    pieces = grouped(refs[: sum(counts)], counts)
    own_ref, odd_refs, even_refs = pieces[0], pieces[1 : size - 1], pieces[size - 1 :]
    grad_refs = views(refs[sum(counts) : -2], places)
    count = len(grad_refs) // 2
    me = lax.axis_index("tensor")
    tokens, rows = x_s.shape[1:]
    own_tokens = tokens // size
    width = out_ref.shape[1] // 2

    def place(ref, slot):
        start = pl.multiple_of(lax.rem(me - slot + size, size) * own_tokens, own_tokens)
        for k in range(count):
            if ref is None:
                values = jnp.zeros((own_tokens, rows), x_s.dtype)
            else:
                part, at = replica_rows(ref, k, own_tokens)
                values = part[at, side * rows : (side + 1) * rows]
            x_s[k, pl.ds(start, own_tokens), :] = values

    place(own_ref, 0)
    for slot, case in enumerate(piece_cases(me, size, even_refs, odd_refs), 1):
        for condition, ref, _ in case:

            @pl.when(condition)
            def _(ref=ref, slot=slot):
                place(ref, slot)

    turned = [x_s[k].T for k in range(count)]
    for j in range(2):
        total = None
        for k in range(count):
            term = jnp.dot(turned[k], grad_refs[j * count + k][...], preferred_element_type=jnp.float32)
            total = term if total is None else total + term
        out_ref[:, j * width : (j + 1) * width] = total


def late_kernel(size, side, counts, places, *refs):
    sum_ref, refs = refs[0], refs[1:]
    out_ref, x_s, last_s, grad_s = refs[-4:]
    pieces = grouped(refs[: sum(counts)], counts)
    own_ref, odd_refs, even_refs = pieces[0], pieces[1:size], pieces[size:]
    grad_refs = views(refs[sum(counts) : -4], places)
    count = len(grad_refs) // 2
    me = lax.axis_index("tensor")
    tokens, rows = x_s.shape
    own_tokens = tokens // size
    width = out_ref.shape[1] // 2
    columns = slice(side * rows, (side + 1) * rows)

    def place(ref, slot):
        start = pl.multiple_of(lax.rem(me - slot + size, size) * own_tokens, own_tokens)
        part, at = replica_rows(ref, count - 1, own_tokens)
        x_s[pl.ds(start, own_tokens), :] = part[at, columns]

    place(own_ref, 0)
    last_s[...] = jnp.zeros_like(last_s)
    for slot, case in enumerate(piece_cases(me, size, even_refs, odd_refs), 1):
        for condition, ref, last in case:

            @pl.when(condition)
            def _(ref=ref, slot=slot, last=last):
                place(ref, slot)
                if last:
                    for k in range(count - 1):
                        part, at = replica_rows(ref, k, own_tokens)
                        last_s[k * own_tokens : (k + 1) * own_tokens, :] = part[at, columns]

    owner = jnp.where(me == 0, size - 1, 0)
    start = pl.multiple_of(owner * own_tokens, own_tokens)
    for j in range(2):
        for k in range(count - 1):
            grad_s[j, k * own_tokens : (k + 1) * own_tokens, :] = grad_refs[j * count + k][pl.ds(start, own_tokens), :]
    turned, last_turned = x_s[...].T, last_s[...].T
    for j in range(2):
        at = slice(j * width, (j + 1) * width)
        total = jnp.dot(turned, grad_refs[j * count + count - 1][...], preferred_element_type=jnp.float32)
        total = total + jnp.dot(last_turned, grad_s[j], preferred_element_type=jnp.float32)
        out_ref[:, at] = (sum_ref[:, at] + total).astype(out_ref.dtype)


def views(refs, places):
    return [refs[which] if half is None else refs[which].at[half] for which, half in places]


def grad_operands(grads):
    arrays, places = [], []
    for array, half in grads:
        if not any(array is a for a in arrays):
            arrays.append(array)
        places.append(([i for i, a in enumerate(arrays) if a is array][0], half))
    return arrays, places


def early_sums(own, even, odd, grads, mirrors, side, size):
    rows = own.shape[1] // mirrors
    grads, places = grad_operands([g for half in grads for g in half[:-1]])
    tokens, width = grads[0].shape[-2:]
    counts = [1] + [len(parts) for parts in odd + even]
    pieces = [own] + [part for parts in odd + even for part in parts]
    return pl.pallas_call(
        functools.partial(early_kernel, size, side, counts, places),
        in_specs=[NEAR] * (len(pieces) + len(grads)),
        out_specs=NEAR,
        out_shape=jax.ShapeDtypeStruct((rows, 2 * width), jnp.float32),
        scratch_shapes=[pltpu.VMEM((len(places) // 2, tokens, rows), jnp.bfloat16)],
        cost_estimate=LENGTHY,
        compiler_params=params(24),
        name="early_sums",
    )(*pieces, *grads)


def late_sums(sums, own, even, odd, grads, mirrors, side, size, dtype):
    rows = own.shape[1] // mirrors
    grads, places = grad_operands([g for half in grads for g in half])
    tokens, width = grads[0].shape[-2:]
    counts = [1] + [len(parts) for parts in odd + even]
    pieces = [sums, own] + [part for parts in odd + even for part in parts]
    last = (len(places) // 2 - 1) * (tokens // size)
    return pl.pallas_call(
        functools.partial(late_kernel, size, side, counts, places),
        in_specs=[NEAR] * (len(pieces) + len(grads)),
        out_specs=NEAR,
        out_shape=jax.ShapeDtypeStruct((rows, 2 * width), dtype),
        scratch_shapes=[
            pltpu.VMEM((tokens, rows), jnp.bfloat16),
            pltpu.VMEM((last, rows), jnp.bfloat16),
            pltpu.VMEM((2, last, width), jnp.bfloat16),
        ],
        cost_estimate=LENGTHY,
        compiler_params=params(24),
        name="late_sums",
    )(*pieces, *grads)


def average_kernel(replicas, own_ref, *refs):
    away_refs, out_ref = refs[:-1], refs[-1]
    total = own_ref[...]
    for away_ref in away_refs:
        total = total + away_ref[...].astype(jnp.float32)
    out_ref[...] = (total * (1.0 / replicas)).reshape(out_ref.shape)


def average(own, away, replicas):
    rows, columns = own.shape
    depth = min(rows, 128)
    block = pl.BlockSpec((depth, columns), lambda i: (i, 0))
    return pl.pallas_call(
        functools.partial(average_kernel, replicas),
        grid=(rows // depth,),
        in_specs=[block] * (1 + len(away)),
        out_specs=pl.BlockSpec((depth, 2, columns // 2), lambda i: (i, 0, 0)),
        out_shape=jax.ShapeDtypeStruct((rows, 2, columns // 2), jnp.float32),
        cost_estimate=BRIEF,
        compiler_params=params(32),
        name="average_weight_grad",
    )(own, *away)


def swap(values, distance, size):
    return lax.ppermute(values, "dp", [(i, i ^ distance) for i in range(size)])


def across(values, distance, size):
    return lax.ppermute(values, "mirror", [(i, (i + distance) % size) for i in range(size)])


def gathered(grads, size):
    bits = [1 << b for b in range(size.bit_length() - 1)]
    near = {bit: swap(grads, bit, size) for bit in bits}
    found = []
    for half, order in enumerate((bits, bits[1:] + bits[:1])):
        blocks = {0: (grads, half)}
        for bit in order:
            for distance, (array, part) in list(blocks.items()):
                if distance == 0:
                    blocks[bit] = (near[bit], half)
                else:
                    moved = array if part is None else array[part]
                    blocks[distance ^ bit] = (swap(moved, bit, size), None)
        found.append([blocks[d] for d in range(size)])
    return found


def shards(layer_input, qk_weight, query_proj, key_proj, value_proj, head_grad, doc_ids):
    size = lax.axis_size("tensor")
    mirrors = lax.axis_size("mirror")
    data_count = lax.axis_size("dp")

    columns = split_columns(layer_input[0], mirrors, data_count)
    columns = [columns[0]] + [swap(columns[d], d, data_count) for d in range(1, data_count)]
    near = 3 * data_count // 4 * (layer_input.shape[2] // data_count)
    grads, weight_rows = attention_grads(
        query_proj[0], key_proj[0], value_proj[0], head_grad[0], doc_ids[0], qk_weight, near
    )
    columns, grads = lax.optimization_barrier((columns, grads))
    piece = merge_tokens(columns)
    partials = input_partials(grads, weight_rows, qk_weight, size, data_count)
    partials = partials.reshape(size, *piece.shape)

    even, odd = [(hop(piece, 0, size, mirrors),)], [(hop(piece, 1, size, mirrors),)]
    own_piece = piece
    for distance in range(size - 1, 0, -1):
        send = {}
        for part in range(PARTS):
            for parity, came in ((0, odd[-1]), (1, even[-1])):
                flow = came[part % len(came)]
                send[parity, part] = pass_on(flow, partials, parity, distance, part, PARTS)
                if distance == 1:
                    send[parity, part], own_piece = lax.optimization_barrier((send[parity, part], own_piece))
        for parity, hops in ((0, even), (1, odd)):
            hops.append(tuple(hop(send[parity, part], parity, size, mirrors) for part in range(PARTS)))

    grads = gathered(grads, data_count)
    sides = range(mirrors)
    early = [early_sums(piece, even[:-2], odd[:-2], grads, mirrors, side, size) for side in sides]
    away = []
    for side in sides[1:]:
        sums = late_sums(early[side], own_piece, even[:-1], odd[:-1], grads, mirrors, side, size, jnp.bfloat16)
        away.append(across(sums, side, mirrors))
    own = late_sums(early[0], own_piece, even[:-1], odd[:-1], grads, mirrors, 0, size, jnp.float32)
    weight_grad = average(own, away, mirrors * data_count)
    last_odd, last_even, weight_grad = lax.optimization_barrier((odd[-1], even[-1], weight_grad))
    input_grad = finish(last_even, last_odd, partials, data_count)[None]
    return (input_grad, weight_grad)


def solution(mesh):
    in_specs = (
        P(("mirror", "dp"), "tensor", None),
        P(None, None, "tensor"),
        P(("mirror", "dp"), None, "tensor"),
        P(("mirror", "dp"), None, "tensor"),
        P(("mirror", "dp"), None, "tensor"),
        P(("mirror", "dp"), None, "tensor"),
        P(("mirror", "dp"), None),
    )
    out_specs = (P(("mirror", "dp"), "tensor", None), P(("mirror", "dp"), None, "tensor"))
    return jax.shard_map(shards, mesh=mesh, in_specs=in_specs, out_specs=out_specs, check_vma=False)
```
